32 devices in a mesh: fsdp: 4 (over x, core), tensor: 8 (over z, y).
Axes of the slice: x: 2, y: 2, z: 4, core: 2. Of those that a mesh axis runs over, the one named last changes fastest.
Arguments:
- weight: bfloat16 [896, 2048], P('tensor', 'fsdp'), may hold values from -0.0017929077 to 0.0017929077
- momentum: float32 [896, 2048], P('tensor', 'fsdp'), may hold values from -18 to 18
- grad: bfloat16 [896, 2048], P('tensor', 'fsdp'), may hold values from -6 to 6
- q_prev: float32 [896, 256], P('tensor'), may hold values from -0.1875 to 0.1875
Outputs:
- new_weight: bfloat16 [896, 2048], P('tensor', 'fsdp')
- new_momentum: float32 [896, 2048], P('tensor', 'fsdp')
- q_new: float32 [896, 256], P('tensor')
The draws below stay inside these ranges and needn't reach their ends.
All inputs are finite; a program needn't handle non-finite values.
Results may differ from the reference program's by a relative error of at most 0.001.
Values sent between devices are 32-bit elements; how exact they have to be, the bound alone decides.
No kernel may reach another device: no remote copies, remote signals or barrier semaphores. Data moves between devices by JAX's collectives and lax.ppermute only.
A program may use at most 64 MiB of HBM per device.

```python
import math
import jax
import jax.numpy as jnp
from jax import lax

RANK = 256
D = 2048
FF = 896


def draw_momentum(key, part):
    position = jnp.arange(FF, dtype=jnp.float32)[:, None] / FF
    base = jnp.clip(jax.random.normal(key, (FF, D), jnp.float32), -6.0, 6.0)
    scale = jnp.exp(position * jnp.log(3.0))
    return base * scale


def level_of(rng, extent, cuts, low, top_value):
    def one(dim, parts):
        draws = jax.random.uniform(jax.random.fold_in(jax.random.fold_in(rng, 6), dim), (parts,), jnp.float32, low / len(cuts), top_value / len(cuts))
        return jnp.repeat(jnp.exp(draws), extent[dim] // parts).reshape((-1,) + (1,) * (len(extent) - dim - 1))

    gain = one(*cuts[0])
    for cut in cuts[1:]:
        gain = gain * one(*cut)
    return gain


def normal_values(key, dims, width, most, shards=(), held_as=jnp.bfloat16):
    entries = jax.random.normal(key, dims, jnp.float32) * width
    if len(shards) > 0:
        entries = level_of(key, dims, shards, -0.22, 0.18) * entries
    return jnp.clip(entries, min=-most, max=most).astype(held_as)


def setup_inputs(seed: int = 0) -> dict:
    seeds = jax.random.split(jax.random.key(seed), 5)
    weight = normal_values(seeds[0], (FF, D), 0.0003, 0.0017929077, ((0, 8), (1, 4)))
    momentum = draw_momentum(jax.random.fold_in(seeds[4], 71), 0)
    grad = normal_values(seeds[2], (FF, D), 1.0, 6.0, ((0, 8), (1, 4)))
    q_prev = normal_values(seeds[3], (FF, RANK), FF ** -0.5, 0.1875, ((0, 8),), jnp.float32)
    return {"weight": weight, "momentum": momentum, "grad": grad, "q_prev": q_prev}


momentum_decay = 0.95
step_rate = 0.02
norm_eps = 1e-06

def reference(weight, momentum, grad, q_prev):
    highest = lax.Precision.HIGHEST
    buffer = momentum + grad.astype(jnp.float32)
    power = lax.dot_general(buffer.astype(jnp.float32), q_prev.astype(jnp.float32), (((0,), (0,)), ((), ())), precision=highest, preferred_element_type=jnp.float32)
    gram = lax.dot_general(power.astype(jnp.float32), power.astype(jnp.float32), (((0,), (0,)), ((), ())), precision=highest, preferred_element_type=jnp.float32)
    lower = jnp.linalg.cholesky(gram)
    ortho = jax.scipy.linalg.solve_triangular(lower, power.T, lower=True).T
    right = jnp.dot(buffer.astype(jnp.float32), ortho.astype(jnp.float32), precision=highest, preferred_element_type=jnp.float32)
    colnorm = jnp.sqrt(lax.optimization_barrier(jnp.sum(right * right, axis=0)))
    q_new = right / (colnorm + norm_eps)
    new_momentum = buffer - (1.0 - momentum_decay) * jnp.dot(right.astype(jnp.float32), ortho.T.astype(jnp.float32), precision=highest, preferred_element_type=jnp.float32)
    factor = step_rate * math.sqrt(FF / D)
    update = jnp.dot(q_new.astype(jnp.float32), ortho.T.astype(jnp.float32), precision=highest, preferred_element_type=jnp.float32)
    new_weight = (weight.astype(jnp.float32) - factor * update).astype(jnp.bfloat16)
    return (new_weight, new_momentum, q_new)
```

```python
import functools
import math

import jax
import jax.numpy as jnp
from jax import lax
from jax.experimental import pallas as pl
from jax.experimental.pallas import tpu as pltpu
from jax.sharding import PartitionSpec as P

momentum_decay = 0.95
step_rate = 0.02
norm_eps = 1e-06
f32 = jnp.float32
bf16 = jnp.bfloat16
block_rows = 16
vmem_bytes = 32 * 1024 * 1024
TT = (((0,), (0,)), ((), ()))
NN = (((1,), (0,)), ((), ()))
NT = (((1,), (1,)), ((), ()))


def split3(x):
    high = x.astype(bf16)
    rest = x - high.astype(f32)
    mid = rest.astype(bf16)
    return high, mid, (rest - mid.astype(f32)).astype(bf16)


def dot6(a, b, dims):
    ah, am, al = split3(a)
    bh, bm, bl = split3(b)

    def one(x, y):
        return lax.dot_general(x, y, dims, preferred_element_type=f32)

    small = one(am, bm) + one(ah, bl) + one(al, bh)
    return one(ah, bh) + (one(ah, bm) + one(am, bh) + small)


def bits_of(size):
    return size.bit_length() - 1


def orders(tensor):
    straight = list(range(bits_of(tensor)))
    other = straight[:]
    if len(straight) > 2:
        other[0], other[1] = other[1], other[0]
    return straight, other


def block_id(tensor):
    mine, core = lax.axis_index("tensor"), lax.axis_index("fsdp") % 2
    kept = bits_of(tensor) - 1
    ids = []
    for order in orders(tensor):
        value = 0
        for step in range(kept):
            bit = (mine // 2 ** order[step]) % 2
            value = value + bit * 2 ** (kept - 1 - step)
        ids.append(value)
    return jnp.where(core == 0, ids[0], ids[1])


def flip_tensor(x, step, fsdp, tensor):
    pairs = []
    for f in range(fsdp):
        bit = orders(tensor)[f % 2][step]
        for t in range(tensor):
            pairs.append((f * tensor + t, f * tensor + (t ^ (1 << bit))))
    return lax.ppermute(x, ("fsdp", "tensor"), pairs)


def flip_fsdp(x, bit, fsdp):
    return lax.ppermute(x, "fsdp", [(f, f ^ (1 << bit)) for f in range(fsdp)])


def call(body, outs, ins, scratch=()):
    shapes = [jax.ShapeDtypeStruct(shape, dtype) for shape, dtype in outs]
    return pl.pallas_call(
        body,
        out_shape=shapes,
        in_specs=[pl.BlockSpec(memory_space=pltpu.VMEM)] * len(ins),
        out_specs=[pl.BlockSpec(memory_space=pltpu.VMEM)] * len(outs),
        scratch_shapes=[pltpu.VMEM(shape, f32) for shape in scratch],
        compiler_params=pltpu.CompilerParams(vmem_limit_bytes=vmem_bytes),
    )(*ins)


def block_at(index, size):
    return pl.ds(pl.multiple_of(index * size, size), size)


def power_kernel(tensor, blocks, mom, grad, q, buf, keep, send, total):
    buffer = mom[...] + grad[...].astype(f32)
    buf[...] = buffer
    total[...] = dot6(buffer, q[...], TT)
    rows = total.shape[0] // blocks
    me = block_id(tensor)
    for j in range(blocks):
        part = total[block_at(me ^ j, rows), :]
        if j < blocks // 2:
            keep[j * rows : (j + 1) * rows, :] = part
        else:
            send[(j - blocks // 2) * rows : (j + 1 - blocks // 2) * rows, :] = part


def cross_kernel(tensor, blocks, count, *refs):
    pieces, buf = refs[:count], refs[count]
    power, keep, send, both = refs[count + 1 :]
    rows = power.shape[0] // blocks
    me = block_id(tensor)
    j = 0
    for piece in pieces:
        for i in range(piece.shape[0] // rows):
            power[block_at(me ^ j, rows), :] = piece[i * rows : (i + 1) * rows, :]
            j += 1
    rank = power.shape[1]
    whole = power[...]
    both[:rank, :] = dot6(whole, whole, TT)
    both[rank:, :] = dot6(buf[...], whole, NN)
    half = both.shape[0] // 2
    core = lax.axis_index("fsdp") % 2
    keep[...] = both[block_at(core, half), :]
    send[...] = both[block_at(1 - core, half), :]


def invert_factor(a):
    size = a.shape[0]
    nb = block_rows
    groups = nb // 8
    lane = lax.broadcasted_iota(jnp.int32, (8, size), 1)
    row = lax.broadcasted_iota(jnp.int32, (8, size), 0)
    row_short = lax.broadcasted_iota(jnp.int32, (8, 128), 0)
    wide = size // 128

    def widen(x):
        return jnp.concatenate([x] * wide, axis=1)

    def spread(x, s):
        return jnp.broadcast_to(x[s : s + 1, :], x.shape)

    for start in range(0, size, nb):
        cols = [
            [
                jnp.broadcast_to(a[start + 8 * g : start + 8 * g + 8, start + j : start + j + 1], (8, 128))
                for g in range(groups)
            ]
            for j in range(nb)
        ]
        panel = []
        for g in range(groups):
            here = (lane >= start) & (lane < start + nb)
            unit = jnp.where(lane - start == row + 8 * g, 1.0, 0.0)
            panel.append(jnp.where(here, unit, a[start + 8 * g : start + 8 * g + 8, :]))
        pivots = [jnp.ones((8, 128), f32) for _ in range(groups)]
        for k in range(nb):
            top, s = divmod(k, 8)
            pivot = spread(cols[k][top], s)
            inverse = 1.0 / pivot
            pivots[top] = jnp.where(row_short == s, pivot, pivots[top])
            lead = spread(panel[top], s)
            leads = [spread(cols[j][top], s) for j in range(nb)]
            for g in range(top, groups):
                factor = cols[k][g] * inverse
                if g == top:
                    if s == 7:
                        continue
                    factor = jnp.where(row_short > s, factor, 0.0)
                for j in range(k + 1, nb):
                    cols[j][g] = cols[j][g] - factor * leads[j]
                panel[g] = panel[g] - widen(factor) * lead
        done = jnp.concatenate([panel[g] * widen(lax.rsqrt(pivots[g])) for g in range(groups)], axis=0)
        a[start : start + nb, :] = done
        below = start + nb
        if below < size:
            h, m, l = split3(done)
            skip = below // 128 * 128
            left = jnp.concatenate([h, h, m, m, h, l], axis=0)[:, skip:]
            right = jnp.concatenate([h, m, h, m, l, h], axis=0)
            change = lax.dot_general(left, right, TT, preferred_element_type=f32)
            lanes = lax.broadcasted_iota(jnp.int32, (size - below, size), 1)
            here = (lanes >= start) & (lanes < below)
            a[below:, :] = jnp.where(here, 0.0, a[below:, :]) - change[below - skip :, :]
    i = lax.broadcasted_iota(jnp.int32, (size, size), 0)
    j = lax.broadcasted_iota(jnp.int32, (size, size), 1)
    a[...] = jnp.where(i >= j, a[...], 0.0)


def factor_kernel(mine, theirs, inverse, right, mixed, squares, both):
    half = mine.shape[0]
    core = lax.axis_index("fsdp") % 2
    both[block_at(core, half), :] = mine[...]
    both[block_at(1 - core, half), :] = theirs[...]
    rank = both.shape[1]
    inverse[...] = both[:rank, :]
    invert_factor(inverse)
    low = inverse[...]
    r = dot6(both[rank:, :], low, NT)
    right[...] = r
    squares[...] = jnp.sum(r * r, axis=0, keepdims=True)
    mixed[...] = dot6(r, low, NN)


def momentum_kernel(buf, mixed, power, out):
    out[...] = buf[...] - (1.0 - momentum_decay) * dot6(mixed[...], power[...], NT)


def weight_kernel(scale, weight, right, squares, inverse, power, out, q_new):
    q = right[...] / (jnp.sqrt(squares[...]) + norm_eps)
    q_new[...] = q
    update = dot6(dot6(q, inverse[...], NN), power[...], NT)
    out[...] = (weight[...].astype(f32) - scale * update).astype(bf16)


def per_device(fsdp, tensor, weight, momentum, grad, q_prev):
    cols, rows = momentum.shape
    rank = q_prev.shape[1]
    scale = step_rate * math.sqrt(cols * tensor / (rows * fsdp))
    steps = bits_of(tensor)
    blocks = 2 ** (steps - 1)
    full = (rows, rank)
    buf, keep, send = call(
        functools.partial(power_kernel, tensor, blocks),
        [((cols, rows), f32), ((rows // 2, rank), f32), ((rows // 2, rank), f32)],
        [momentum, grad, q_prev],
        [full],
    )
    for step in range(steps - 1):
        total = keep + flip_tensor(send, step, fsdp, tensor)
        half = total.shape[0] // 2
        if step < steps - 2:
            send, keep = total[half:], total[:half]
    total = total + flip_tensor(total, steps - 1, fsdp, tensor)
    pieces = [total]
    for step in reversed(range(steps - 1)):
        came = flip_tensor(total, step, fsdp, tensor)
        pieces.append(came)
        if step > 0:
            total = jnp.concatenate([total, came], axis=0)
    half = (rank + cols) // 2
    power, keep, send = call(
        functools.partial(cross_kernel, tensor, blocks, len(pieces)),
        [(full, f32), ((half, rank), f32), ((half, rank), f32)],
        [*pieces, buf],
        [(rank + cols, rank)],
    )
    mine = keep + flip_fsdp(send, 0, fsdp)
    for bit in range(1, bits_of(fsdp)):
        mine = mine + flip_fsdp(mine, bit, fsdp)
    theirs = flip_fsdp(mine, 0, fsdp)
    inverse, right, mixed, squares = call(
        factor_kernel,
        [((rank, rank), f32), ((cols, rank), f32), ((cols, rank), f32), ((1, rank), f32)],
        [mine, theirs],
        [(rank + cols, rank)],
    )
    (new_momentum,) = call(momentum_kernel, [((cols, rows), f32)], [buf, mixed, power])
    for step in range(steps):
        squares = squares + flip_tensor(squares, step, fsdp, tensor)
    new_weight, q_new = call(
        functools.partial(weight_kernel, scale),
        [((cols, rows), bf16), ((cols, rank), f32)],
        [weight, right, squares, inverse, power],
    )
    return (new_weight, new_momentum, q_new)


def solution(mesh):
    placed = (P("tensor", "fsdp"), P("tensor", "fsdp"), P("tensor", "fsdp"), P("tensor", None))
    return jax.shard_map(
        functools.partial(per_device, mesh.shape["fsdp"], mesh.shape["tensor"]),
        mesh=mesh,
        in_specs=placed,
        out_specs=(P("tensor", "fsdp"), P("tensor", "fsdp"), P("tensor", None)),
        check_vma=False,
    )
```

```python
import functools
import math

import jax
import jax.numpy as jnp
from jax import lax
from jax.experimental import pallas as pl
from jax.experimental.pallas import tpu as pltpu
from jax.sharding import PartitionSpec as P

momentum_decay = 0.95
step_rate = 0.02
norm_eps = 1e-06
f32 = jnp.float32
bf16 = jnp.bfloat16
block_rows = 16
vmem_bytes = 32 * 1024 * 1024
TT = (((0,), (0,)), ((), ()))
NN = (((1,), (0,)), ((), ()))
NT = (((1,), (1,)), ((), ()))


def split3(x):
    high = x.astype(bf16)
    rest = x - high.astype(f32)
    mid = rest.astype(bf16)
    return high, mid, (rest - mid.astype(f32)).astype(bf16)


def dot6(a, b, dims):
    ah, am, al = split3(a)
    bh, bm, bl = split3(b)

    def one(x, y):
        return lax.dot_general(x, y, dims, preferred_element_type=f32)

    small = one(am, bm) + one(ah, bl) + one(al, bh)
    return one(ah, bh) + (one(ah, bm) + one(am, bh) + small)


def bits_of(size):
    return size.bit_length() - 1


def partner(core, j):
    return ((0, 1, 2, 3), (0, 2, 1, 3))[core][j]


def block_of(j):
    mine, core = lax.axis_index("tensor") % 4, lax.axis_index("fsdp") % 2
    return jnp.where(core == 0, mine ^ partner(0, j), mine ^ partner(1, j))


def to_partner(x, j, fsdp, tensor):
    pairs = []
    for f in range(fsdp):
        for t in range(tensor):
            pairs.append((f * tensor + t, f * tensor + (t ^ partner(f % 2, j))))
    return lax.ppermute(x, ("fsdp", "tensor"), pairs)


def flip_tensor(x, bit, tensor):
    return lax.ppermute(x, "tensor", [(t, t ^ (1 << bit)) for t in range(tensor)])


def flip_fsdp(x, bit, fsdp):
    return lax.ppermute(x, "fsdp", [(f, f ^ (1 << bit)) for f in range(fsdp)])


def flip_across(x, f_flip, t_flip, fsdp, tensor):
    pairs = []
    for f in range(fsdp):
        for t in range(tensor):
            pairs.append((f * tensor + t, (f ^ 1 ^ f_flip) * tensor + (t ^ t_flip)))
    return lax.ppermute(x, ("fsdp", "tensor"), pairs)


def call(body, outs, ins, scratch=(), micros=1):
    shapes = [jax.ShapeDtypeStruct(shape, dtype) for shape, dtype in outs]
    return pl.pallas_call(
        body,
        out_shape=shapes,
        in_specs=[pl.BlockSpec(memory_space=pltpu.VMEM)] * len(ins),
        out_specs=[pl.BlockSpec(memory_space=pltpu.VMEM)] * len(outs),
        scratch_shapes=[pltpu.VMEM(shape, f32) for shape in scratch],
        compiler_params=pltpu.CompilerParams(vmem_limit_bytes=vmem_bytes),
        cost_estimate=pl.CostEstimate(flops=int(micros * 1e9), bytes_accessed=0, transcendentals=0),
    )(*ins)


def block_at(index, size):
    return pl.ds(pl.multiple_of(index * size, size), size)


def power_kernel(mom_in, grad_in, q_in, buf, *refs):
    parts, (total, mom, grad, q, sems) = refs[:4], refs[4:]
    copies = [
        pltpu.make_async_copy(src, dst, sems.at[i])
        for i, (src, dst) in enumerate(((mom_in, mom), (grad_in, grad), (q_in, q)))
    ]
    for copy in copies:
        copy.start()
    for copy in copies:
        copy.wait()
    buffer = mom[...] + grad[...].astype(f32)
    buf[...] = buffer
    total[...] = dot6(buffer, q[...], TT)
    rows = total.shape[0] // 4
    for j in range(4):
        parts[j][...] = total[block_at(block_of(j), rows), :]


def first_gram_kernel(p0, p1, p2, p3, power, first):
    rows = power.shape[0] // 4
    half = first.shape[0]
    for j, piece in enumerate((p0, p1, p2, p3)):
        power[block_at(block_of(j), rows), :] = piece[...]
    left = power[:, :half]
    first[...] = dot6(left, left, TT)


def cross_kernel(power, buf, second, third):
    whole = power[...]
    half = second.shape[1]
    second[...] = dot6(whole, whole[:, half:], TT)
    third[...] = dot6(buf[...], whole, NN)


def invert_factor(a):
    size = a.shape[0]
    nb = block_rows
    groups = nb // 8
    lane = lax.broadcasted_iota(jnp.int32, (8, size), 1)
    row = lax.broadcasted_iota(jnp.int32, (8, size), 0)
    row_short = lax.broadcasted_iota(jnp.int32, (8, 128), 0)
    wide = size // 128

    def widen(x):
        return jnp.concatenate([x] * wide, axis=1)

    def spread(x, s):
        return jnp.broadcast_to(x[s : s + 1, :], x.shape)

    for start in range(0, size, nb):
        cols = [
            [
                jnp.broadcast_to(a[start + 8 * g : start + 8 * g + 8, start + j : start + j + 1], (8, 128))
                for g in range(groups)
            ]
            for j in range(nb)
        ]
        panel = []
        for g in range(groups):
            here = (lane >= start) & (lane < start + nb)
            unit = jnp.where(lane - start == row + 8 * g, 1.0, 0.0)
            panel.append(jnp.where(here, unit, a[start + 8 * g : start + 8 * g + 8, :]))
        pivots = [jnp.ones((8, 128), f32) for _ in range(groups)]
        for k in range(nb):
            top, s = divmod(k, 8)
            pivot = spread(cols[k][top], s)
            inverse = 1.0 / pivot
            pivots[top] = jnp.where(row_short == s, pivot, pivots[top])
            lead = spread(panel[top], s)
            leads = [spread(cols[j][top], s) for j in range(nb)]
            for g in range(top, groups):
                factor = cols[k][g] * inverse
                if g == top:
                    if s == 7:
                        continue
                    factor = jnp.where(row_short > s, factor, 0.0)
                for j in range(k + 1, nb):
                    cols[j][g] = cols[j][g] - factor * leads[j]
                panel[g] = panel[g] - widen(factor) * lead
        done = jnp.concatenate([panel[g] * widen(lax.rsqrt(pivots[g])) for g in range(groups)], axis=0)
        a[start : start + nb, :] = done
        below = start + nb
        if below < size:
            h, m, l = split3(done)
            skip = below // 128 * 128
            left = jnp.concatenate([h, h, m, m, h, l], axis=0)[:, skip:]
            right = jnp.concatenate([h, m, h, m, l, h], axis=0)
            change = lax.dot_general(left, right, TT, preferred_element_type=f32)
            lanes = lax.broadcasted_iota(jnp.int32, (size - below, size), 1)
            here = (lanes >= start) & (lanes < below)
            a[below:, :] = jnp.where(here, 0.0, a[below:, :]) - change[below - skip :, :]
    i = lax.broadcasted_iota(jnp.int32, (size, size), 0)
    j = lax.broadcasted_iota(jnp.int32, (size, size), 1)
    a[...] = jnp.where(i >= j, a[...], 0.0)


def first_kernel(gram, came, inverse):
    inverse[...] = gram[...] + came[...]
    invert_factor(inverse)


def second_kernel(rest, came, inverse1, inverse, corner):
    half = inverse1.shape[0]
    inv1 = inverse1[...]
    upper = dot6(inv1, rest[:half, :] + came[:half, :], NN)
    corner[...] = rest[half:, :] + came[half:, :] - dot6(upper, upper, TT)
    invert_factor(corner)
    inv2 = corner[...]
    inverse[:half, :half] = inv1
    inverse[:half, half:] = jnp.zeros_like(inv1)
    inverse[half:, :half] = -dot6(inv2, dot6(upper, inv1, TT), NN)
    inverse[half:, half:] = inv2


def right_kernel(cross, came, inverse, right, squares):
    r = dot6(cross[...] + came[...], inverse[...], NT)
    right[...] = r
    squares[...] = jnp.sum(r * r, axis=0, keepdims=True)


def ortho_kernel(power, inverse, ortho):
    ortho[...] = dot6(power[...], inverse[...], NT)


def momentum_kernel(buf, right, ortho, out):
    out[...] = buf[...] - (1.0 - momentum_decay) * dot6(right[...], ortho[...], NT)


def weight_kernel(scale, weight, right, squares, ortho, out, q_new):
    q = right[...] / (jnp.sqrt(squares[...]) + norm_eps)
    q_new[...] = q
    update = dot6(q, ortho[...], NT)
    out[...] = (weight[...].astype(f32) - scale * update).astype(bf16)


def per_device(fsdp, tensor, weight, momentum, grad, q_prev):
    cols, rows = momentum.shape
    rank = q_prev.shape[1]
    half = rank // 2
    scale = step_rate * math.sqrt(cols * tensor / (rows * fsdp))
    block = ((rows // 4, rank), f32)
    buf, *parts = pl.pallas_call(
        power_kernel,
        out_shape=[jax.ShapeDtypeStruct(*x) for x in [((cols, rows), f32), block, block, block, block]],
        in_specs=[pl.BlockSpec(memory_space=pltpu.HBM)] * 3,
        out_specs=[pl.BlockSpec(memory_space=pltpu.VMEM)] * 5,
        scratch_shapes=[
            pltpu.VMEM((rows, rank), f32),
            pltpu.VMEM((cols, rows), f32),
            pltpu.VMEM((cols, rows), bf16),
            pltpu.VMEM((cols, rank), f32),
            pltpu.SemaphoreType.DMA((3,)),
        ],
        compiler_params=pltpu.CompilerParams(vmem_limit_bytes=vmem_bytes),
    )(*[pltpu.with_memory_space_constraint(x, pltpu.HBM) for x in (momentum, grad, q_prev)])
    came = [to_partner(parts[j], j, fsdp, tensor) for j in (1, 2, 3)]
    total = parts[0] + came[0] + came[1] + came[2]
    for bit in range(2, bits_of(tensor)):
        total = total + flip_tensor(total, bit, tensor)
    pieces = [total] + [to_partner(total, j, fsdp, tensor) for j in (1, 2, 3)]
    power, first = call(first_gram_kernel, [((rows, rank), f32), ((half, half), f32)], pieces)
    second, third = call(cross_kernel, [((rank, half), f32), ((cols, rank), f32)], [power, buf])
    came = [flip_fsdp(x, 0, fsdp) for x in (first, second, third)]
    first, second, third = first + came[0], second + came[1], third + came[2]
    first, second, third = lax.optimization_barrier((first, second, third))
    for bit in range(1, bits_of(fsdp) - 1):
        first, second, third = [x + flip_across(x, 1 << bit, 0, fsdp, tensor) for x in (first, second, third)]
    came = [flip_across(x, fsdp // 2, 0, fsdp, tensor) for x in (first, second, third)]
    (inverse1,) = call(first_kernel, [((half, half), f32)], [first, came[0]], micros=4)
    (inverse,) = call(second_kernel, [((rank, rank), f32)], [second, came[1], inverse1], [(half, half)], micros=4)
    right, squares = call(right_kernel, [((cols, rank), f32), ((1, rank), f32)], [third, came[2], inverse])
    (ortho,) = call(ortho_kernel, [((rows, rank), f32)], [power, inverse], micros=2)
    (new_momentum,) = call(momentum_kernel, [((cols, rows), f32)], [buf, right, ortho], micros=2)
    for bit in range(bits_of(tensor)):
        if bit == bits_of(tensor) - 1:
            squares, ortho = lax.optimization_barrier((squares, ortho))
        squares = squares + flip_across(squares, 0, 1 << bit, fsdp, tensor)
    new_weight, q_new = call(
        functools.partial(weight_kernel, scale),
        [((cols, rows), bf16), ((cols, rank), f32)],
        [weight, right, squares, ortho],
    )
    return (new_weight, new_momentum, q_new)


def solution(mesh):
    placed = (P("tensor", "fsdp"), P("tensor", "fsdp"), P("tensor", "fsdp"), P("tensor", None))
    return jax.shard_map(
        functools.partial(per_device, mesh.shape["fsdp"], mesh.shape["tensor"]),
        mesh=mesh,
        in_specs=placed,
        out_specs=(P("tensor", "fsdp"), P("tensor", "fsdp"), P("tensor", None)),
        check_vma=False,
    )
```

```python
import functools
import math

import jax
import jax.numpy as jnp
from jax import lax
from jax.experimental import pallas as pl
from jax.experimental.pallas import tpu as pltpu
from jax.sharding import PartitionSpec as P

momentum_decay = 0.95
step_rate = 0.02
norm_eps = 1e-06
f32 = jnp.float32
bf16 = jnp.bfloat16
block_rows = 32
step_rows = 16
vmem_bytes = 32 * 1024 * 1024
TT = (((0,), (0,)), ((), ()))
NN = (((1,), (0,)), ((), ()))
NT = (((1,), (1,)), ((), ()))


def split3(x):
    high = x.astype(bf16)
    rest = x - high.astype(f32)
    mid = rest.astype(bf16)
    return high, mid, (rest - mid.astype(f32)).astype(bf16)


def dot6(a, b, dims):
    ah, am, al = split3(a)
    bh, bm, bl = split3(b)

    def one(x, y):
        return lax.dot_general(x, y, dims, preferred_element_type=f32)

    small = one(am, bm) + one(ah, bl) + one(al, bh)
    return one(ah, bh) + (one(ah, bm) + one(am, bh) + small)


def bits_of(size):
    return size.bit_length() - 1


def partner(core, j):
    return ((0, 1, 2, 3), (0, 2, 1, 3))[core][j]


def block_of(j):
    mine, core = lax.axis_index("tensor") % 4, lax.axis_index("fsdp") % 2
    return jnp.where(core == 0, mine ^ partner(0, j), mine ^ partner(1, j))


def to_partner(x, j, fsdp, tensor):
    pairs = []
    for f in range(fsdp):
        for t in range(tensor):
            pairs.append((f * tensor + t, f * tensor + (t ^ partner(f % 2, j))))
    return lax.ppermute(x, ("fsdp", "tensor"), pairs)


def flip_tensor(x, bit, tensor):
    return lax.ppermute(x, "tensor", [(t, t ^ (1 << bit)) for t in range(tensor)])


def flip_fsdp(x, bit, fsdp):
    return lax.ppermute(x, "fsdp", [(f, f ^ (1 << bit)) for f in range(fsdp)])


def flip_across(x, f_flip, t_flip, fsdp, tensor):
    pairs = []
    for f in range(fsdp):
        for t in range(tensor):
            pairs.append((f * tensor + t, (f ^ 1 ^ f_flip) * tensor + (t ^ t_flip)))
    return lax.ppermute(x, ("fsdp", "tensor"), pairs)


def call(body, outs, ins, scratch=(), micros=1):
    shapes = [jax.ShapeDtypeStruct(shape, dtype) for shape, dtype in outs]
    return pl.pallas_call(
        body,
        out_shape=shapes,
        in_specs=[pl.BlockSpec(memory_space=pltpu.VMEM)] * len(ins),
        out_specs=[pl.BlockSpec(memory_space=pltpu.VMEM)] * len(outs),
        scratch_shapes=[pltpu.VMEM(shape, f32) for shape in scratch],
        compiler_params=pltpu.CompilerParams(vmem_limit_bytes=vmem_bytes),
        cost_estimate=pl.CostEstimate(flops=int(micros * 1e9), bytes_accessed=0, transcendentals=0),
    )(*ins)


def block_at(index, size):
    return pl.ds(pl.multiple_of(index * size, size), size)


def power_kernel(mom_in, grad_in, q_in, buf, *refs):
    parts, (total, mom, grad, q, sems) = refs[:8], refs[8:]
    copies = [
        pltpu.make_async_copy(src, dst, sems.at[i])
        for i, (src, dst) in enumerate(((mom_in, mom), (grad_in, grad), (q_in, q)))
    ]
    for copy in copies:
        copy.start()
    for copy in copies:
        copy.wait()
    buffer = mom[...] + grad[...].astype(f32)
    buf[...] = buffer
    total[...] = dot6(buffer, q[...], TT)
    rows = total.shape[0] // 4
    half = total.shape[1] // 2
    for j in range(4):
        here = block_at(block_of(j), rows)
        parts[j][...] = total[here, :half]
        parts[4 + j][...] = total[here, half:]


def gather_blocks(pieces, out):
    rows = out.shape[0] // 4
    for j, piece in enumerate(pieces):
        out[block_at(block_of(j), rows), :] = piece[...]


def first_gram_kernel(p0, p1, p2, p3, left, first):
    gather_blocks((p0, p1, p2, p3), left)
    first[...] = dot6(left[...], left[...], TT)


def cross_kernel(p0, p1, p2, p3, left, buf, power, second, third, right):
    gather_blocks((p0, p1, p2, p3), right)
    whole = jnp.concatenate([left[...], right[...]], axis=1)
    power[...] = whole
    second[...] = dot6(whole, right[...], TT)
    third[...] = dot6(buf[...], whole, NN)


def invert_factor(a):
    size = a.shape[0]
    groups = block_rows // 8
    lane = lax.broadcasted_iota(jnp.int32, (8, size), 1)
    row = lax.broadcasted_iota(jnp.int32, (8, size), 0)
    row_short = lax.broadcasted_iota(jnp.int32, (8, 128), 0)
    wide = size // 128

    def widen(x):
        return jnp.concatenate([x] * wide, axis=1) if wide > 1 else x

    def spread(x, s):
        return jnp.broadcast_to(x[s : s + 1, :], x.shape)

    for start in range(0, size, block_rows):
        panel = [a[start + 8 * g : start + 8 * g + 8, :] for g in range(groups)]
        pivots = [jnp.ones((8, 128), f32) for _ in range(groups)]
        for done in range(0, block_rows, step_rows):
            first = start + done
            cols = [
                {g: jnp.broadcast_to(panel[g][:, first + j : first + j + 1], (8, 128)) for g in range(done // 8, groups)}
                for j in range(step_rows)
            ]
            for g in range(groups):
                here = (lane >= first) & (lane < first + step_rows)
                panel[g] = jnp.where(here, jnp.where(lane - start == row + 8 * g, 1.0, 0.0), panel[g])
            for k in range(step_rows):
                top, s = divmod(done + k, 8)
                leads = {j: spread(cols[j][top], s) for j in range(k, step_rows)}
                inverse = 1.0 / leads[k]
                pivots[top] = jnp.where(row_short == s, leads[k], pivots[top])
                lead = spread(panel[top], s)
                for g in range(top, groups):
                    if g == top and s == 7:
                        continue
                    factor = cols[k][g] * inverse
                    for j in range(k + 1, step_rows):
                        cols[j][g] = cols[j][g] - factor * leads[j]
                    if g == top:
                        factor = jnp.where(row_short > s, factor, 0.0)
                    panel[g] = panel[g] - widen(factor) * lead
        rows = jnp.concatenate([panel[g] * widen(lax.rsqrt(pivots[g])) for g in range(groups)], axis=0)
        below = start + block_rows
        a[start:below, :] = rows
        if below < size:
            h, m, l = split3(rows)
            skip = below // 128 * 128
            left = jnp.concatenate([h, h, m, m, h, l], axis=0)[:, skip:]
            right = jnp.concatenate([h, m, h, m, l, h], axis=0)
            change = lax.dot_general(left, right, TT, preferred_element_type=f32)
            lanes = lax.broadcasted_iota(jnp.int32, (size - below, size), 1)
            here = (lanes >= start) & (lanes < below)
            a[below:, :] = jnp.where(here, 0.0, a[below:, :]) - change[below - skip :, :]
    i = lax.broadcasted_iota(jnp.int32, (size, size), 0)
    j = lax.broadcasted_iota(jnp.int32, (size, size), 1)
    a[...] = jnp.where(i >= j, a[...], 0.0)


def first_kernel(gram, came, inverse):
    inverse[...] = gram[...] + came[...]
    invert_factor(inverse)


def second_kernel(rest, came, inverse1, inverse, corner):
    half = inverse1.shape[0]
    inv1 = inverse1[...]
    upper = dot6(inv1, rest[:half, :] + came[:half, :], NN)
    corner[...] = rest[half:, :] + came[half:, :] - dot6(upper, upper, TT)
    below = dot6(upper, inv1, TT)
    invert_factor(corner)
    inv2 = corner[...]
    inverse[:half, :half] = inv1
    inverse[:half, half:] = jnp.zeros_like(inv1)
    inverse[half:, :half] = -dot6(inv2, below, NN)
    inverse[half:, half:] = inv2


def right_kernel(cross, came, inverse, right, squares):
    r = dot6(cross[...] + came[...], inverse[...], NT)
    right[...] = r
    squares[...] = jnp.sum(r * r, axis=0, keepdims=True)


def ortho_kernel(power, inverse, ortho, high, mid):
    o = dot6(power[...], inverse[...], NT)
    ortho[...] = o
    high[...], mid[...], _ = split3(o)


def momentum_kernel(buf, right, ortho, out):
    out[...] = buf[...] - (1.0 - momentum_decay) * dot6(right[...], ortho[...], NT)


def weight_kernel(scale, weight, right, squares, high, mid, out, q_new):
    q = right[...] / (jnp.sqrt(squares[...]) + norm_eps)
    q_new[...] = q
    qh, qm, _ = split3(q)

    def one(x, y):
        return lax.dot_general(x, y[...], NT, preferred_element_type=f32)

    update = one(qh, high) + (one(qh, mid) + one(qm, high) + one(qm, mid))
    out[...] = (weight[...].astype(f32) - scale * update).astype(bf16)


def per_device(fsdp, tensor, weight, momentum, grad, q_prev):
    cols, rows = momentum.shape
    rank = q_prev.shape[1]
    half = rank // 2
    scale = step_rate * math.sqrt(cols * tensor / (rows * fsdp))
    block = ((rows // 4, half), f32)
    buf, *parts = pl.pallas_call(
        power_kernel,
        out_shape=[jax.ShapeDtypeStruct(*x) for x in [((cols, rows), f32)] + [block] * 8],
        in_specs=[pl.BlockSpec(memory_space=pltpu.HBM)] * 3,
        out_specs=[pl.BlockSpec(memory_space=pltpu.VMEM)] * 9,
        scratch_shapes=[
            pltpu.VMEM((rows, rank), f32),
            pltpu.VMEM((cols, rows), f32),
            pltpu.VMEM((cols, rows), bf16),
            pltpu.VMEM((cols, rank), f32),
            pltpu.SemaphoreType.DMA((3,)),
        ],
        compiler_params=pltpu.CompilerParams(vmem_limit_bytes=vmem_bytes),
    )(*[pltpu.with_memory_space_constraint(x, pltpu.HBM) for x in (momentum, grad, q_prev)])
    totals = []
    for mine in (parts[:4], parts[4:]):
        came = [to_partner(mine[j], j, fsdp, tensor) for j in (1, 2, 3)]
        totals.append(mine[0] + came[0] + came[1] + came[2])
    for bit in range(2, bits_of(tensor)):
        totals = [x + flip_tensor(x, bit, tensor) for x in totals]
    pieces = [[x] + [to_partner(x, j, fsdp, tensor) for j in (1, 2, 3)] for x in totals]
    left, first = call(first_gram_kernel, [((rows, half), f32), ((half, half), f32)], pieces[0])
    power, second, third = call(
        cross_kernel,
        [((rows, rank), f32), ((rank, half), f32), ((cols, rank), f32)],
        [*pieces[1], left, buf],
        [(rows, half)],
    )
    first = first + flip_fsdp(first, 0, fsdp)
    came = [flip_fsdp(x, 0, fsdp) for x in (second, third)]
    second, third = lax.optimization_barrier((second + came[0], third + came[1]))
    for bit in range(1, bits_of(fsdp) - 1):
        first, second, third = [x + flip_across(x, 1 << bit, 0, fsdp, tensor) for x in (first, second, third)]
    came = [flip_across(x, fsdp // 2, 0, fsdp, tensor) for x in (first, second, third)]
    (inverse1,) = call(first_kernel, [((half, half), f32)], [first, came[0]], micros=4)
    (inverse,) = call(second_kernel, [((rank, rank), f32)], [second, came[1], inverse1], [(half, half)], micros=4)
    right, squares = call(right_kernel, [((cols, rank), f32), ((1, rank), f32)], [third, came[2], inverse])
    ortho, high, mid = call(
        ortho_kernel,
        [((rows, rank), f32), ((rows, rank), bf16), ((rows, rank), bf16)],
        [power, inverse],
    )
    (new_momentum,) = call(momentum_kernel, [((cols, rows), f32)], [buf, right, ortho], micros=2)
    came = [flip_across(squares, 0, j, fsdp, tensor) for j in (1, 2, 3)]
    squares = squares + came[0] + came[1] + came[2]
    squares, ortho = lax.optimization_barrier((squares, ortho))
    for bit in range(2, bits_of(tensor)):
        squares = squares + flip_across(squares, 0, 1 << bit, fsdp, tensor)
    new_weight, q_new = call(
        functools.partial(weight_kernel, scale),
        [((cols, rows), bf16), ((cols, rank), f32)],
        [weight, right, squares, high, mid],
    )
    return (new_weight, new_momentum, q_new)


def solution(mesh):
    placed = (P("tensor", "fsdp"), P("tensor", "fsdp"), P("tensor", "fsdp"), P("tensor", None))
    return jax.shard_map(
        functools.partial(per_device, mesh.shape["fsdp"], mesh.shape["tensor"]),
        mesh=mesh,
        in_specs=placed,
        out_specs=(P("tensor", "fsdp"), P("tensor", "fsdp"), P("tensor", None)),
        check_vma=False,
    )
```

```python
import functools
import math

import jax
import jax.numpy as jnp
from jax import lax
from jax.experimental import pallas as pl
from jax.experimental.pallas import tpu as pltpu
from jax.sharding import PartitionSpec as P

momentum_decay = 0.95
step_rate = 0.02
norm_eps = 1e-06
f32 = jnp.float32
bf16 = jnp.bfloat16
block_rows = 32
step_rows = 16
vmem_bytes = 32 * 1024 * 1024
TT = (((0,), (0,)), ((), ()))
NN = (((1,), (0,)), ((), ()))
NT = (((1,), (1,)), ((), ()))


def split3(x):
    high = x.astype(bf16)
    rest = x - high.astype(f32)
    mid = rest.astype(bf16)
    return high, mid, (rest - mid.astype(f32)).astype(bf16)


def dot6(a, b, dims):
    ah, am, al = split3(a)
    bh, bm, bl = split3(b)
    (a_dim,), (b_dim,) = dims[0]
    left = jnp.concatenate([ah, ah, am, am, ah, al], axis=a_dim)
    right = jnp.concatenate([bh, bm, bh, bm, bl, bh], axis=b_dim)
    return lax.dot_general(left, right, dims, preferred_element_type=f32)


def bits_of(size):
    return size.bit_length() - 1


def partner(core, j):
    return ((0, 3, 1, 2), (0, 3, 2, 1))[core][j]


def block_of(j):
    mine, core = lax.axis_index("tensor") % 4, lax.axis_index("fsdp") % 2
    return jnp.where(core == 0, mine ^ partner(0, j), mine ^ partner(1, j))


def to_partner(x, j, fsdp, tensor):
    pairs = []
    for f in range(fsdp):
        for t in range(tensor):
            pairs.append((f * tensor + t, f * tensor + (t ^ partner(f % 2, j))))
    return lax.ppermute(x, ("fsdp", "tensor"), pairs)


def flip_tensor(x, bit, tensor):
    return lax.ppermute(x, "tensor", [(t, t ^ (1 << bit)) for t in range(tensor)])


def flip_fsdp(x, bit, fsdp):
    return lax.ppermute(x, "fsdp", [(f, f ^ (1 << bit)) for f in range(fsdp)])


def flip_across(x, f_flip, t_flip, fsdp, tensor):
    pairs = []
    for f in range(fsdp):
        for t in range(tensor):
            pairs.append((f * tensor + t, (f ^ 1 ^ f_flip) * tensor + (t ^ t_flip)))
    return lax.ppermute(x, ("fsdp", "tensor"), pairs)


def call(body, outs, ins, scratch=(), micros=1):
    shapes = [jax.ShapeDtypeStruct(shape, dtype) for shape, dtype in outs]
    return pl.pallas_call(
        body,
        out_shape=shapes,
        in_specs=[pl.BlockSpec(memory_space=pltpu.VMEM)] * len(ins),
        out_specs=[pl.BlockSpec(memory_space=pltpu.VMEM)] * len(outs),
        scratch_shapes=[pltpu.VMEM(shape, f32) for shape in scratch],
        compiler_params=pltpu.CompilerParams(vmem_limit_bytes=vmem_bytes),
        cost_estimate=pl.CostEstimate(flops=int(micros * 1e9), bytes_accessed=0, transcendentals=0),
    )(*ins)


def block_at(index, size):
    return pl.ds(pl.multiple_of(index * size, size), size)


def power_kernel(mom_in, grad_in, q_in, buf, *refs):
    parts, (total, mom, grad, q, sems) = refs[:8], refs[8:]
    copies = [
        pltpu.make_async_copy(src, dst, sems.at[i])
        for i, (src, dst) in enumerate(((mom_in, mom), (grad_in, grad), (q_in, q)))
    ]
    for copy in copies:
        copy.start()
    for copy in copies:
        copy.wait()
    buffer = mom[...] + grad[...].astype(f32)
    buf[...] = buffer
    total[...] = dot6(q[...], buffer, TT)
    half = total.shape[0] // 2
    for j in range(4):
        here = block_at(block_of(j), total.shape[1] // 4)
        parts[j][...] = total[:half, here]
        parts[4 + j][...] = total[half:, here]


def gather_blocks(pieces, out):
    for j, piece in enumerate(pieces):
        out[:, block_at(block_of(j), out.shape[1] // 4)] = piece[...]


def first_gram_kernel(p0, p1, p2, p3, upper, first):
    gather_blocks((p0, p1, p2, p3), upper)
    first[...] = dot6(upper[...], upper[...], NT)


def second_gram_kernel(p0, p1, p2, p3, upper, lower, second):
    gather_blocks((p0, p1, p2, p3), lower)
    half = lower.shape[0]
    second[:, :half] = dot6(lower[...], upper[...], NT)
    second[:, half:] = dot6(lower[...], lower[...], NT)


def cross_kernel(upper, lower, buf, third):
    half = lower.shape[0]
    third[:, :half] = dot6(buf[...], upper[...], NT)
    third[:, half:] = dot6(buf[...], lower[...], NT)


def invert_factor(a):
    size = a.shape[0]
    groups = block_rows // 8
    lane = lax.broadcasted_iota(jnp.int32, (8, size), 1)
    row = lax.broadcasted_iota(jnp.int32, (8, size), 0)
    row_short = lax.broadcasted_iota(jnp.int32, (8, 128), 0)
    wide = size // 128

    def widen(x):
        return jnp.concatenate([x] * wide, axis=1) if wide > 1 else x

    def spread(x, s):
        return jnp.broadcast_to(x[s : s + 1, :], x.shape)

    for start in range(0, size, block_rows):
        panel = [a[start + 8 * g : start + 8 * g + 8, :] for g in range(groups)]
        pivots = [jnp.ones((8, 128), f32) for _ in range(groups)]
        for done in range(0, block_rows, step_rows):
            first = start + done
            cols = [
                {g: jnp.broadcast_to(panel[g][:, first + j : first + j + 1], (8, 128)) for g in range(done // 8, groups)}
                for j in range(step_rows)
            ]
            for g in range(groups):
                here = (lane >= first) & (lane < first + step_rows)
                panel[g] = jnp.where(here, jnp.where(lane - start == row + 8 * g, 1.0, 0.0), panel[g])
            for k in range(step_rows):
                top, s = divmod(done + k, 8)
                leads = {j: spread(cols[j][top], s) for j in range(k, step_rows)}
                inverse = 1.0 / leads[k]
                pivots[top] = jnp.where(row_short == s, leads[k], pivots[top])
                lead = spread(panel[top], s)
                for g in range(top, groups):
                    if g == top and s == 7:
                        continue
                    factor = cols[k][g] * inverse
                    for j in range(k + 1, step_rows):
                        cols[j][g] = cols[j][g] - factor * leads[j]
                    if g == top:
                        factor = jnp.where(row_short > s, factor, 0.0)
                    panel[g] = panel[g] - widen(factor) * lead
        rows = jnp.concatenate([panel[g] * widen(lax.rsqrt(pivots[g])) for g in range(groups)], axis=0)
        below = start + block_rows
        a[start:below, :] = rows
        if below < size:
            h, m, l = split3(rows)
            skip = below // 128 * 128
            left = jnp.concatenate([h, h, m, m, h, l], axis=0)[:, skip:]
            right = jnp.concatenate([h, m, h, m, l, h], axis=0)
            change = lax.dot_general(left, right, TT, preferred_element_type=f32)
            lanes = lax.broadcasted_iota(jnp.int32, (size - below, size), 1)
            here = (lanes >= start) & (lanes < below)
            a[below:, :] = jnp.where(here, 0.0, a[below:, :]) - change[below - skip :, :]
    i = lax.broadcasted_iota(jnp.int32, (size, size), 0)
    j = lax.broadcasted_iota(jnp.int32, (size, size), 1)
    a[...] = jnp.where(i >= j, a[...], 0.0)


def first_kernel(gram, came, inverse):
    inverse[...] = gram[...] + came[...]
    invert_factor(inverse)


def second_kernel(rest, came, inverse1, inverse, corner):
    half = inverse1.shape[0]
    inv1 = inverse1[...]
    gram = rest[...] + came[...]
    low = dot6(gram[:, :half], inv1, NT)
    corner[...] = gram[:, half:] - dot6(low, low, NT)
    below = dot6(low, inv1, NN)
    invert_factor(corner)
    inv2 = corner[...]
    inverse[:half, :half] = inv1
    inverse[:half, half:] = jnp.zeros_like(inv1)
    inverse[half:, :half] = -dot6(inv2, below, NN)
    inverse[half:, half:] = inv2


def right_kernel(cross, came, inverse, right, squares):
    r = dot6(cross[...] + came[...], inverse[...], NT)
    right[...] = r
    squares[...] = jnp.sum(r * r, axis=0, keepdims=True)


def ortho_kernel(upper, lower, inverse, ortho, high, mid):
    o = dot6(inverse[...], jnp.concatenate([upper[...], lower[...]], axis=0), NN)
    ortho[...] = o
    high[...], mid[...], _ = split3(o)


def momentum_kernel(buf, right, ortho, out):
    out[...] = buf[...] - (1.0 - momentum_decay) * dot6(right[...], ortho[...], NN)


def weight_kernel(scale, weight, right, squares, high, mid, out, q_new):
    q = right[...] / (jnp.sqrt(squares[...]) + norm_eps)
    q_new[...] = q
    qh, qm, _ = split3(q)

    def one(x, y):
        return lax.dot_general(x, y[...], NN, preferred_element_type=f32)

    update = one(qh, high) + (one(qh, mid) + one(qm, high) + one(qm, mid))
    out[...] = (weight[...].astype(f32) - scale * update).astype(bf16)


def per_device(fsdp, tensor, weight, momentum, grad, q_prev):
    cols, rows = momentum.shape
    rank = q_prev.shape[1]
    half = rank // 2
    scale = step_rate * math.sqrt(cols * tensor / (rows * fsdp))
    block = ((half, rows // 4), f32)
    buf, *parts = pl.pallas_call(
        power_kernel,
        out_shape=[jax.ShapeDtypeStruct(*x) for x in [((cols, rows), f32)] + [block] * 8],
        in_specs=[pl.BlockSpec(memory_space=pltpu.HBM)] * 3,
        out_specs=[pl.BlockSpec(memory_space=pltpu.VMEM)] * 9,
        scratch_shapes=[
            pltpu.VMEM((rank, rows), f32),
            pltpu.VMEM((cols, rows), f32),
            pltpu.VMEM((cols, rows), bf16),
            pltpu.VMEM((cols, rank), f32),
            pltpu.SemaphoreType.DMA((3,)),
        ],
        compiler_params=pltpu.CompilerParams(vmem_limit_bytes=vmem_bytes),
    )(*[pltpu.with_memory_space_constraint(x, pltpu.HBM) for x in (momentum, grad, q_prev)])
    totals = []
    for mine in (parts[:4], parts[4:]):
        came = [to_partner(mine[j], j, fsdp, tensor) for j in (1, 2, 3)]
        totals.append(mine[0] + came[0] + came[1] + came[2])
    for bit in range(2, bits_of(tensor)):
        totals = [x + flip_tensor(x, bit, tensor) for x in totals]
    pieces = [[x] + [to_partner(x, j, fsdp, tensor) for j in (1, 2, 3)] for x in totals]
    upper, first = call(first_gram_kernel, [((half, rows), f32), ((half, half), f32)], pieces[0])
    lower, second = call(second_gram_kernel, [((half, rows), f32), ((half, rank), f32)], [*pieces[1], upper])
    (third,) = call(cross_kernel, [((cols, rank), f32)], [upper, lower, buf])
    first = first + flip_fsdp(first, 0, fsdp)
    came = [flip_fsdp(x, 0, fsdp) for x in (second, third)]
    second, third = lax.optimization_barrier((second + came[0], third + came[1]))
    for bit in range(1, bits_of(fsdp) - 1):
        first, second, third = [x + flip_across(x, 1 << bit, 0, fsdp, tensor) for x in (first, second, third)]
    came = [flip_across(x, fsdp // 2, 0, fsdp, tensor) for x in (first, second, third)]
    (inverse1,) = call(first_kernel, [((half, half), f32)], [first, came[0]], micros=4)
    (inverse,) = call(second_kernel, [((rank, rank), f32)], [second, came[1], inverse1], [(half, half)], micros=4)
    right, squares = call(right_kernel, [((cols, rank), f32), ((1, rank), f32)], [third, came[2], inverse])
    ortho, high, mid = call(
        ortho_kernel,
        [((rank, rows), f32), ((rank, rows), bf16), ((rank, rows), bf16)],
        [upper, lower, inverse],
    )
    (new_momentum,) = call(momentum_kernel, [((cols, rows), f32)], [buf, right, ortho], micros=2)
    came = [flip_across(squares, 0, j, fsdp, tensor) for j in (3, 1, 2)]
    squares = squares + came[0] + came[1] + came[2]
    squares, ortho = lax.optimization_barrier((squares, ortho))
    for bit in range(2, bits_of(tensor)):
        squares = squares + flip_across(squares, 0, 1 << bit, fsdp, tensor)
    new_weight, q_new = call(
        functools.partial(weight_kernel, scale),
        [((cols, rows), bf16), ((cols, rank), f32)],
        [weight, right, squares, high, mid],
    )
    return (new_weight, new_momentum, q_new)


def solution(mesh):
    placed = (P("tensor", "fsdp"), P("tensor", "fsdp"), P("tensor", "fsdp"), P("tensor", None))
    return jax.shard_map(
        functools.partial(per_device, mesh.shape["fsdp"], mesh.shape["tensor"]),
        mesh=mesh,
        in_specs=placed,
        out_specs=(P("tensor", "fsdp"), P("tensor", "fsdp"), P("tensor", None)),
        check_vma=False,
    )
```

```python
import functools
import math

import jax
import jax.numpy as jnp
from jax import lax
from jax.experimental import pallas as pl
from jax.experimental.pallas import tpu as pltpu
from jax.sharding import PartitionSpec as P

momentum_decay = 0.95
step_rate = 0.02
norm_eps = 1e-06
f32 = jnp.float32
bf16 = jnp.bfloat16
block_rows = 32
step_rows = 16
vmem_bytes = 32 * 1024 * 1024
TT = (((0,), (0,)), ((), ()))
NN = (((1,), (0,)), ((), ()))
NT = (((1,), (1,)), ((), ()))


def split3(x):
    high = x.astype(bf16)
    rest = x - high.astype(f32)
    mid = rest.astype(bf16)
    return high, mid, (rest - mid.astype(f32)).astype(bf16)


def dot6(a, b, dims):
    ah, am, al = split3(a)
    bh, bm, bl = split3(b)
    (a_dim,), (b_dim,) = dims[0]
    left = jnp.concatenate([ah, ah, am, am, ah, al], axis=a_dim)
    right = jnp.concatenate([bh, bm, bh, bm, bl, bh], axis=b_dim)
    return lax.dot_general(left, right, dims, preferred_element_type=f32)


def bits_of(size):
    return size.bit_length() - 1


def partner(j):
    return (0, 3, 1, 2)[j]


def block_of(j):
    return (lax.axis_index("tensor") % 4) ^ partner(j)


def to_partner(x, j, tensor):
    return lax.ppermute(x, "tensor", [(t, t ^ partner(j)) for t in range(tensor)])


def flip_tensor(x, bit, tensor):
    return lax.ppermute(x, "tensor", [(t, t ^ (1 << bit)) for t in range(tensor)])


def flip_fsdp(x, bit, fsdp):
    return lax.ppermute(x, "fsdp", [(f, f ^ (1 << bit)) for f in range(fsdp)])


def flip_across(x, f_flip, t_flip, fsdp, tensor):
    pairs = []
    for f in range(fsdp):
        for t in range(tensor):
            pairs.append((f * tensor + t, (f ^ 1 ^ f_flip) * tensor + (t ^ t_flip)))
    return lax.ppermute(x, ("fsdp", "tensor"), pairs)


def call(body, outs, ins, scratch=(), micros=1):
    shapes = [jax.ShapeDtypeStruct(shape, dtype) for shape, dtype in outs]
    return pl.pallas_call(
        body,
        out_shape=shapes,
        in_specs=[pl.BlockSpec(memory_space=pltpu.VMEM)] * len(ins),
        out_specs=[pl.BlockSpec(memory_space=pltpu.VMEM)] * len(outs),
        scratch_shapes=[pltpu.VMEM(shape, f32) for shape in scratch],
        compiler_params=pltpu.CompilerParams(vmem_limit_bytes=vmem_bytes),
        cost_estimate=pl.CostEstimate(flops=int(micros * 1e9), bytes_accessed=0, transcendentals=0),
    )(*ins)


def block_at(index, size):
    return pl.ds(pl.multiple_of(index * size, size), size)


def power_kernel(mom_in, grad_in, q_in, buf, *refs):
    parts, (total, mom, grad, q, sems) = refs[:8], refs[8:]
    copies = [
        pltpu.make_async_copy(src, dst, sems.at[i])
        for i, (src, dst) in enumerate(((mom_in, mom), (grad_in, grad), (q_in, q)))
    ]
    for copy in copies:
        copy.start()
    for copy in copies:
        copy.wait()
    buffer = mom[...] + grad[...].astype(f32)
    buf[...] = buffer
    total[...] = dot6(q[...], buffer, TT)
    half = total.shape[0] // 2
    for j in range(4):
        here = block_at(block_of(j), total.shape[1] // 4)
        parts[j][...] = total[:half, here]
        parts[4 + j][...] = total[half:, here]


def gather_blocks(pieces, out):
    for j, piece in enumerate(pieces):
        out[:, block_at(block_of(j), out.shape[1] // 4)] = piece[...]


def first_gram_kernel(p0, p1, p2, p3, upper, first):
    gather_blocks((p0, p1, p2, p3), upper)
    first[...] = dot6(upper[...], upper[...], NT)


def second_gram_kernel(p0, p1, p2, p3, upper, lower, second):
    gather_blocks((p0, p1, p2, p3), lower)
    half = lower.shape[0]
    second[:, :half] = dot6(lower[...], upper[...], NT)
    second[:, half:] = dot6(lower[...], lower[...], NT)


def cross_kernel(upper, lower, buf, third):
    half = lower.shape[0]
    third[:, :half] = dot6(buf[...], upper[...], NT)
    third[:, half:] = dot6(buf[...], lower[...], NT)


def invert_factor(a):
    size = a.shape[0]
    groups = block_rows // 8
    lane = lax.broadcasted_iota(jnp.int32, (8, size), 1)
    row = lax.broadcasted_iota(jnp.int32, (8, size), 0)
    row_short = lax.broadcasted_iota(jnp.int32, (8, 128), 0)
    wide = size // 128

    def widen(x):
        return jnp.concatenate([x] * wide, axis=1) if wide > 1 else x

    def spread(x, s):
        return jnp.broadcast_to(x[s : s + 1, :], x.shape)

    for start in range(0, size, block_rows):
        panel = [a[start + 8 * g : start + 8 * g + 8, :] for g in range(groups)]
        pivots = [jnp.ones((8, 128), f32) for _ in range(groups)]
        for done in range(0, block_rows, step_rows):
            first = start + done
            cols = [
                {g: jnp.broadcast_to(panel[g][:, first + j : first + j + 1], (8, 128)) for g in range(done // 8, groups)}
                for j in range(step_rows)
            ]
            for g in range(groups):
                here = (lane >= first) & (lane < first + step_rows)
                panel[g] = jnp.where(here, jnp.where(lane - start == row + 8 * g, 1.0, 0.0), panel[g])
            for k in range(step_rows):
                top, s = divmod(done + k, 8)
                leads = {j: spread(cols[j][top], s) for j in range(k, step_rows)}
                inverse = 1.0 / leads[k]
                pivots[top] = jnp.where(row_short == s, leads[k], pivots[top])
                lead = spread(panel[top], s)
                for g in range(top, groups):
                    if g == top and s == 7:
                        continue
                    factor = cols[k][g] * inverse
                    for j in range(k + 1, step_rows):
                        cols[j][g] = cols[j][g] - factor * leads[j]
                    if g == top:
                        factor = jnp.where(row_short > s, factor, 0.0)
                    panel[g] = panel[g] - widen(factor) * lead
        rows = jnp.concatenate([panel[g] * widen(lax.rsqrt(pivots[g])) for g in range(groups)], axis=0)
        below = start + block_rows
        a[start:below, :] = rows
        if below < size:
            h, m, l = split3(rows)
            skip = below // 128 * 128
            left = jnp.concatenate([h, h, m, m, h, l], axis=0)[:, skip:]
            right = jnp.concatenate([h, m, h, m, l, h], axis=0)
            change = lax.dot_general(left, right, TT, preferred_element_type=f32)
            lanes = lax.broadcasted_iota(jnp.int32, (size - below, size), 1)
            here = (lanes >= start) & (lanes < below)
            a[below:, :] = jnp.where(here, 0.0, a[below:, :]) - change[below - skip :, :]
    i = lax.broadcasted_iota(jnp.int32, (size, size), 0)
    j = lax.broadcasted_iota(jnp.int32, (size, size), 1)
    a[...] = jnp.where(i >= j, a[...], 0.0)


def first_kernel(gram, came, inverse):
    inverse[...] = gram[...] + came[...]
    invert_factor(inverse)


def second_kernel(rest, came, inverse1, inverse, corner):
    half = inverse1.shape[0]
    inv1 = inverse1[...]
    gram = rest[...] + came[...]
    low = dot6(gram[:, :half], inv1, NT)
    corner[...] = gram[:, half:] - dot6(low, low, NT)
    below = dot6(low, inv1, NN)
    invert_factor(corner)
    inv2 = corner[...]
    inverse[:half, :half] = inv1
    inverse[:half, half:] = jnp.zeros_like(inv1)
    inverse[half:, :half] = -dot6(inv2, below, NN)
    inverse[half:, half:] = inv2


def right_kernel(cross, came, inverse, right, squares):
    r = dot6(cross[...] + came[...], inverse[...], NT)
    right[...] = r
    squares[...] = jnp.sum(r * r, axis=0, keepdims=True)


def ortho_kernel(upper, lower, inverse, ortho, high, mid):
    o = dot6(inverse[...], jnp.concatenate([upper[...], lower[...]], axis=0), NN)
    ortho[...] = o
    high[...], mid[...], _ = split3(o)


def momentum_kernel(buf, right, ortho, out):
    out[...] = buf[...] - (1.0 - momentum_decay) * dot6(right[...], ortho[...], NN)


def weight_kernel(scale, weight, right, squares, high, mid, out, q_new):
    q = right[...] / (jnp.sqrt(squares[...]) + norm_eps)
    q_new[...] = q
    qh, qm, _ = split3(q)

    def one(x, y):
        return lax.dot_general(x, y[...], NN, preferred_element_type=f32)

    update = one(qh, high) + (one(qh, mid) + one(qm, high) + one(qm, mid))
    out[...] = (weight[...].astype(f32) - scale * update).astype(bf16)


def per_device(fsdp, tensor, weight, momentum, grad, q_prev):
    cols, rows = momentum.shape
    rank = q_prev.shape[1]
    half = rank // 2
    scale = step_rate * math.sqrt(cols * tensor / (rows * fsdp))
    block = ((half, rows // 4), f32)
    buf, *parts = pl.pallas_call(
        power_kernel,
        out_shape=[jax.ShapeDtypeStruct(*x) for x in [((cols, rows), f32)] + [block] * 8],
        in_specs=[pl.BlockSpec(memory_space=pltpu.HBM)] * 3,
        out_specs=[pl.BlockSpec(memory_space=pltpu.VMEM)] * 9,
        scratch_shapes=[
            pltpu.VMEM((rank, rows), f32),
            pltpu.VMEM((cols, rows), f32),
            pltpu.VMEM((cols, rows), bf16),
            pltpu.VMEM((cols, rank), f32),
            pltpu.SemaphoreType.DMA((3,)),
        ],
        compiler_params=pltpu.CompilerParams(vmem_limit_bytes=vmem_bytes),
    )(*[pltpu.with_memory_space_constraint(x, pltpu.HBM) for x in (momentum, grad, q_prev)])
    totals = []
    for mine in (parts[:4], parts[4:]):
        came = [to_partner(mine[j], j, tensor) for j in (1, 2, 3)]
        totals.append(mine[0] + came[0] + came[1] + came[2])
    for bit in range(2, bits_of(tensor)):
        totals = [x + flip_tensor(x, bit, tensor) for x in totals]
    pieces = [[x] + [to_partner(x, j, tensor) for j in (1, 2, 3)] for x in totals]
    upper, first = call(first_gram_kernel, [((half, rows), f32), ((half, half), f32)], pieces[0])
    lower, second = call(second_gram_kernel, [((half, rows), f32), ((half, rank), f32)], [*pieces[1], upper])
    (third,) = call(cross_kernel, [((cols, rank), f32)], [upper, lower, buf])
    first = first + flip_fsdp(first, 0, fsdp)
    came = [flip_fsdp(x, 0, fsdp) for x in (second, third)]
    second, third = lax.optimization_barrier((second + came[0], third + came[1]))
    for bit in range(1, bits_of(fsdp) - 1):
        first, second, third = [x + flip_across(x, 1 << bit, 0, fsdp, tensor) for x in (first, second, third)]
    came = [flip_across(x, fsdp // 2, 0, fsdp, tensor) for x in (first, second, third)]
    (inverse1,) = call(first_kernel, [((half, half), f32)], [first, came[0]], micros=4)
    (inverse,) = call(second_kernel, [((rank, rank), f32)], [second, came[1], inverse1], [(half, half)], micros=4)
    right, squares = call(right_kernel, [((cols, rank), f32), ((1, rank), f32)], [third, came[2], inverse])
    ortho, high, mid = call(
        ortho_kernel,
        [((rank, rows), f32), ((rank, rows), bf16), ((rank, rows), bf16)],
        [upper, lower, inverse],
    )
    (new_momentum,) = call(momentum_kernel, [((cols, rows), f32)], [buf, right, ortho], micros=2)
    came = [flip_across(squares, 0, j, fsdp, tensor) for j in (3, 1, 2)]
    squares = squares + came[0] + came[1] + came[2]
    squares, ortho = lax.optimization_barrier((squares, ortho))
    for bit in range(2, bits_of(tensor)):
        squares = squares + flip_across(squares, 0, 1 << bit, fsdp, tensor)
    new_weight, q_new = call(
        functools.partial(weight_kernel, scale),
        [((cols, rows), bf16), ((cols, rank), f32)],
        [weight, right, squares, high, mid],
    )
    return (new_weight, new_momentum, q_new)


def solution(mesh):
    placed = (P("tensor", "fsdp"), P("tensor", "fsdp"), P("tensor", "fsdp"), P("tensor", None))
    return jax.shard_map(
        functools.partial(per_device, mesh.shape["fsdp"], mesh.shape["tensor"]),
        mesh=mesh,
        in_specs=placed,
        out_specs=(P("tensor", "fsdp"), P("tensor", "fsdp"), P("tensor", None)),
        check_vma=False,
    )
```

```python
import functools
import math

import jax
import jax.numpy as jnp
from jax import lax
from jax.experimental import pallas as pl
from jax.experimental.pallas import tpu as pltpu
from jax.sharding import PartitionSpec as P

momentum_decay = 0.95
step_rate = 0.02
norm_eps = 1e-06
f32 = jnp.float32
bf16 = jnp.bfloat16
block_rows = 32
step_rows = 16
vmem_bytes = 32 * 1024 * 1024
TT = (((0,), (0,)), ((), ()))
NN = (((1,), (0,)), ((), ()))
NT = (((1,), (1,)), ((), ()))


def split3(x):
    high = x.astype(bf16)
    rest = x - high.astype(f32)
    mid = rest.astype(bf16)
    return high, mid, (rest - mid.astype(f32)).astype(bf16)


def dot6(a, b, dims):
    ah, am, al = split3(a)
    bh, bm, bl = split3(b)
    (a_dim,), (b_dim,) = dims[0]
    left = jnp.concatenate([ah, ah, am, am, ah, al], axis=a_dim)
    right = jnp.concatenate([bh, bm, bh, bm, bl, bh], axis=b_dim)
    return lax.dot_general(left, right, dims, preferred_element_type=f32)


def bits_of(size):
    return size.bit_length() - 1


def partner(j):
    return (0, 3, 1, 2)[j]


def block_of(j):
    return (lax.axis_index("tensor") % 4) ^ partner(j)


def to_partner(x, j, tensor):
    return lax.ppermute(x, "tensor", [(t, t ^ partner(j)) for t in range(tensor)])


def flip_tensor(x, bit, tensor):
    return lax.ppermute(x, "tensor", [(t, t ^ (1 << bit)) for t in range(tensor)])


def flip_fsdp(x, bit, fsdp):
    return lax.ppermute(x, "fsdp", [(f, f ^ (1 << bit)) for f in range(fsdp)])


def flip_across(x, f_flip, t_flip, fsdp, tensor):
    pairs = []
    for f in range(fsdp):
        for t in range(tensor):
            pairs.append((f * tensor + t, (f ^ 1 ^ f_flip) * tensor + (t ^ t_flip)))
    return lax.ppermute(x, ("fsdp", "tensor"), pairs)


def call(body, outs, ins, scratch=(), micros=1):
    shapes = [jax.ShapeDtypeStruct(shape, dtype) for shape, dtype in outs]
    return pl.pallas_call(
        body,
        out_shape=shapes,
        in_specs=[pl.BlockSpec(memory_space=pltpu.VMEM)] * len(ins),
        out_specs=[pl.BlockSpec(memory_space=pltpu.VMEM)] * len(outs),
        scratch_shapes=[pltpu.VMEM(shape, f32) for shape in scratch],
        compiler_params=pltpu.CompilerParams(vmem_limit_bytes=vmem_bytes),
        cost_estimate=pl.CostEstimate(flops=int(micros * 1e9), bytes_accessed=0, transcendentals=0),
    )(*ins)


def block_at(index, size):
    return pl.ds(pl.multiple_of(index * size, size), size)


def power_kernel(mom_in, grad_in, q_in, buf, *refs):
    parts, (total, mom, grad, q, sems) = refs[:8], refs[8:]
    copies = [
        pltpu.make_async_copy(src, dst, sems.at[i])
        for i, (src, dst) in enumerate(((mom_in, mom), (grad_in, grad), (q_in, q)))
    ]
    for copy in copies:
        copy.start()
    for copy in copies:
        copy.wait()
    buffer = mom[...] + grad[...].astype(f32)
    buf[...] = buffer
    total[...] = dot6(q[...], buffer, TT)
    half = total.shape[0] // 2
    for j in range(4):
        here = block_at(block_of(j), total.shape[1] // 4)
        parts[j][...] = total[:half, here]
        parts[4 + j][...] = total[half:, here]


def gather_blocks(pieces, out):
    for j, piece in enumerate(pieces):
        out[:, block_at(block_of(j), out.shape[1] // 4)] = piece[...]


def first_gram_kernel(p0, p1, p2, p3, upper, first):
    gather_blocks((p0, p1, p2, p3), upper)
    first[...] = dot6(upper[...], upper[...], NT)


def second_gram_kernel(p0, p1, p2, p3, upper, lower, second):
    gather_blocks((p0, p1, p2, p3), lower)
    half = lower.shape[0]
    second[:, :half] = dot6(lower[...], upper[...], NT)
    second[:, half:] = dot6(lower[...], lower[...], NT)


def first_cross_kernel(upper, buf, cross):
    cross[...] = dot6(buf[...], upper[...], NT)


def cross_kernel(lower, buf, cross, third):
    half = lower.shape[0]
    third[:, :half] = cross[...]
    third[:, half:] = dot6(buf[...], lower[...], NT)


def invert_factor(a):
    size = a.shape[0]
    groups = block_rows // 8
    lane = lax.broadcasted_iota(jnp.int32, (8, size), 1)
    row = lax.broadcasted_iota(jnp.int32, (8, size), 0)
    row_short = lax.broadcasted_iota(jnp.int32, (8, 128), 0)
    wide = size // 128

    def widen(x):
        return jnp.concatenate([x] * wide, axis=1) if wide > 1 else x

    def spread(x, s):
        return jnp.broadcast_to(x[s : s + 1, :], x.shape)

    for start in range(0, size, block_rows):
        panel = [a[start + 8 * g : start + 8 * g + 8, :] for g in range(groups)]
        pivots = [jnp.ones((8, 128), f32) for _ in range(groups)]
        for done in range(0, block_rows, step_rows):
            first = start + done
            cols = [
                {g: jnp.broadcast_to(panel[g][:, first + j : first + j + 1], (8, 128)) for g in range(done // 8, groups)}
                for j in range(step_rows)
            ]
            for g in range(groups):
                here = (lane >= first) & (lane < first + step_rows)
                panel[g] = jnp.where(here, jnp.where(lane - start == row + 8 * g, 1.0, 0.0), panel[g])
            for k in range(step_rows):
                top, s = divmod(done + k, 8)
                leads = {j: spread(cols[j][top], s) for j in range(k, step_rows)}
                inverse = 1.0 / leads[k]
                pivots[top] = jnp.where(row_short == s, leads[k], pivots[top])
                lead = spread(panel[top], s)
                for g in range(top, groups):
                    if g == top and s == 7:
                        continue
                    factor = cols[k][g] * inverse
                    for j in range(k + 1, step_rows):
                        cols[j][g] = cols[j][g] - factor * leads[j]
                    if g == top:
                        factor = jnp.where(row_short > s, factor, 0.0)
                    panel[g] = panel[g] - widen(factor) * lead
        rows = jnp.concatenate([panel[g] * widen(lax.rsqrt(pivots[g])) for g in range(groups)], axis=0)
        below = start + block_rows
        a[start:below, :] = rows
        if below < size:
            h, m, l = split3(rows)
            skip = below // 128 * 128
            left = jnp.concatenate([h, h, m, m, h, l], axis=0)[:, skip:]
            right = jnp.concatenate([h, m, h, m, l, h], axis=0)
            change = lax.dot_general(left, right, TT, preferred_element_type=f32)
            lanes = lax.broadcasted_iota(jnp.int32, (size - below, size), 1)
            here = (lanes >= start) & (lanes < below)
            a[below:, :] = jnp.where(here, 0.0, a[below:, :]) - change[below - skip :, :]
    i = lax.broadcasted_iota(jnp.int32, (size, size), 0)
    j = lax.broadcasted_iota(jnp.int32, (size, size), 1)
    a[...] = jnp.where(i >= j, a[...], 0.0)


def first_kernel(gram, came, inverse):
    inverse[...] = gram[...] + came[...]
    invert_factor(inverse)


def second_kernel(rest, came, inverse1, inverse, corner):
    half = inverse1.shape[0]
    inv1 = inverse1[...]
    gram = rest[...] + came[...]
    low = dot6(gram[:, :half], inv1, NT)
    corner[...] = gram[:, half:] - dot6(low, low, NT)
    below = dot6(low, inv1, NN)
    invert_factor(corner)
    inv2 = corner[...]
    inverse[:half, :half] = inv1
    inverse[:half, half:] = jnp.zeros_like(inv1)
    inverse[half:, :half] = -dot6(inv2, below, NN)
    inverse[half:, half:] = inv2


def right_kernel(cross, came, inverse, right, squares):
    r = dot6(cross[...] + came[...], inverse[...], NT)
    right[...] = r
    squares[...] = jnp.sum(r * r, axis=0, keepdims=True)


def ortho_kernel(upper, lower, inverse, ortho, high, mid):
    o = dot6(inverse[...], jnp.concatenate([upper[...], lower[...]], axis=0), NN)
    ortho[...] = o
    high[...], mid[...], _ = split3(o)


def momentum_kernel(buf, right, ortho, out):
    out[...] = buf[...] - (1.0 - momentum_decay) * dot6(right[...], ortho[...], NN)


def weight_kernel(scale, weight, right, squares, high, mid, out, q_new):
    q = right[...] / (jnp.sqrt(squares[...]) + norm_eps)
    q_new[...] = q
    qh, qm, _ = split3(q)

    def one(x, y):
        return lax.dot_general(x, y[...], NN, preferred_element_type=f32)

    update = one(qh, high) + (one(qh, mid) + one(qm, high) + one(qm, mid))
    out[...] = (weight[...].astype(f32) - scale * update).astype(bf16)


def per_device(fsdp, tensor, weight, momentum, grad, q_prev):
    cols, rows = momentum.shape
    rank = q_prev.shape[1]
    half = rank // 2
    scale = step_rate * math.sqrt(cols * tensor / (rows * fsdp))
    block = ((half, rows // 4), f32)
    buf, *parts = pl.pallas_call(
        power_kernel,
        out_shape=[jax.ShapeDtypeStruct(*x) for x in [((cols, rows), f32)] + [block] * 8],
        in_specs=[pl.BlockSpec(memory_space=pltpu.HBM)] * 3,
        out_specs=[pl.BlockSpec(memory_space=pltpu.VMEM)] * 9,
        scratch_shapes=[
            pltpu.VMEM((rank, rows), f32),
            pltpu.VMEM((cols, rows), f32),
            pltpu.VMEM((cols, rows), bf16),
            pltpu.VMEM((cols, rank), f32),
            pltpu.SemaphoreType.DMA((3,)),
        ],
        compiler_params=pltpu.CompilerParams(vmem_limit_bytes=vmem_bytes),
    )(*[pltpu.with_memory_space_constraint(x, pltpu.HBM) for x in (momentum, grad, q_prev)])
    totals = []
    for mine in (parts[:4], parts[4:]):
        came = [to_partner(mine[j], j, tensor) for j in (1, 2, 3)]
        totals.append(mine[0] + came[0] + came[1] + came[2])
    for bit in range(2, bits_of(tensor)):
        totals = [x + flip_tensor(x, bit, tensor) for x in totals]
    pieces = [[x] + [to_partner(x, j, tensor) for j in (1, 2, 3)] for x in totals]
    upper, first = call(first_gram_kernel, [((half, rows), f32), ((half, half), f32)], pieces[0])
    (cross,) = call(first_cross_kernel, [((cols, half), f32)], [upper, buf])
    cross, upper = lax.optimization_barrier((cross, upper))
    lower, second = call(second_gram_kernel, [((half, rows), f32), ((half, rank), f32)], [*pieces[1], upper])
    (third,) = call(cross_kernel, [((cols, rank), f32)], [lower, buf, cross])
    first = first + flip_fsdp(first, 0, fsdp)
    came = [flip_fsdp(x, 0, fsdp) for x in (second, third)]
    second, third = lax.optimization_barrier((second + came[0], third + came[1]))
    for bit in range(1, bits_of(fsdp) - 1):
        first, second, third = [x + flip_across(x, 1 << bit, 0, fsdp, tensor) for x in (first, second, third)]
    came = [flip_across(x, fsdp // 2, 0, fsdp, tensor) for x in (first, second, third)]
    (inverse1,) = call(first_kernel, [((half, half), f32)], [first, came[0]], micros=4)
    (inverse,) = call(second_kernel, [((rank, rank), f32)], [second, came[1], inverse1], [(half, half)], micros=4)
    right, squares = call(right_kernel, [((cols, rank), f32), ((1, rank), f32)], [third, came[2], inverse])
    ortho, high, mid = call(
        ortho_kernel,
        [((rank, rows), f32), ((rank, rows), bf16), ((rank, rows), bf16)],
        [upper, lower, inverse],
    )
    (new_momentum,) = call(momentum_kernel, [((cols, rows), f32)], [buf, right, ortho], micros=2)
    came = [flip_across(squares, 0, j, fsdp, tensor) for j in (3, 1, 2)]
    squares = squares + came[0] + came[1] + came[2]
    squares, ortho = lax.optimization_barrier((squares, ortho))
    for bit in range(2, bits_of(tensor)):
        squares = squares + flip_across(squares, 0, 1 << bit, fsdp, tensor)
    new_weight, q_new = call(
        functools.partial(weight_kernel, scale),
        [((cols, rows), bf16), ((cols, rank), f32)],
        [weight, right, squares, high, mid],
    )
    return (new_weight, new_momentum, q_new)


def solution(mesh):
    placed = (P("tensor", "fsdp"), P("tensor", "fsdp"), P("tensor", "fsdp"), P("tensor", None))
    return jax.shard_map(
        functools.partial(per_device, mesh.shape["fsdp"], mesh.shape["tensor"]),
        mesh=mesh,
        in_specs=placed,
        out_specs=(P("tensor", "fsdp"), P("tensor", "fsdp"), P("tensor", None)),
        check_vma=False,
    )
```

```python
import functools
import math

import jax
import jax.numpy as jnp
from jax import lax
from jax.experimental import pallas as pl
from jax.experimental.pallas import tpu as pltpu
from jax.sharding import PartitionSpec as P

momentum_decay = 0.95
step_rate = 0.02
norm_eps = 1e-06
f32 = jnp.float32
bf16 = jnp.bfloat16
block_rows = 32
step_rows = 16
vmem_bytes = 32 * 1024 * 1024
TT = (((0,), (0,)), ((), ()))
NN = (((1,), (0,)), ((), ()))
NT = (((1,), (1,)), ((), ()))


def split3(x):
    high = x.astype(bf16)
    rest = x - high.astype(f32)
    mid = rest.astype(bf16)
    return high, mid, (rest - mid.astype(f32)).astype(bf16)


def dot6(a, b, dims):
    ah, am, al = split3(a)
    bh, bm, bl = split3(b)
    (a_dim,), (b_dim,) = dims[0]
    left = jnp.concatenate([ah, ah, am, am, ah, al], axis=a_dim)
    right = jnp.concatenate([bh, bm, bh, bm, bl, bh], axis=b_dim)
    return lax.dot_general(left, right, dims, preferred_element_type=f32)


def bits_of(size):
    return size.bit_length() - 1


def partner(j):
    return (0, 3, 1, 2)[j]


def block_of(j):
    return (lax.axis_index("tensor") % 4) ^ partner(j)


def to_partner(x, j, tensor):
    return lax.ppermute(x, "tensor", [(t, t ^ partner(j)) for t in range(tensor)])


def flip_tensor(x, bit, tensor):
    return lax.ppermute(x, "tensor", [(t, t ^ (1 << bit)) for t in range(tensor)])


def flip_fsdp(x, bit, fsdp):
    return lax.ppermute(x, "fsdp", [(f, f ^ (1 << bit)) for f in range(fsdp)])


def flip_across(x, f_flip, t_flip, fsdp, tensor):
    pairs = []
    for f in range(fsdp):
        for t in range(tensor):
            pairs.append((f * tensor + t, (f ^ 1 ^ f_flip) * tensor + (t ^ t_flip)))
    return lax.ppermute(x, ("fsdp", "tensor"), pairs)


def call(body, outs, ins, scratch=(), micros=1):
    shapes = [jax.ShapeDtypeStruct(shape, dtype) for shape, dtype in outs]
    return pl.pallas_call(
        body,
        out_shape=shapes,
        in_specs=[pl.BlockSpec(memory_space=pltpu.VMEM)] * len(ins),
        out_specs=[pl.BlockSpec(memory_space=pltpu.VMEM)] * len(outs),
        scratch_shapes=[pltpu.VMEM(shape, f32) for shape in scratch],
        compiler_params=pltpu.CompilerParams(vmem_limit_bytes=vmem_bytes),
        cost_estimate=pl.CostEstimate(flops=int(micros * 1e9), bytes_accessed=0, transcendentals=0),
    )(*ins)


def block_at(index, size):
    return pl.ds(pl.multiple_of(index * size, size), size)


def power_kernel(mom_in, grad_in, q_in, buf, *refs):
    parts, (total, mom, grad, q, sems) = refs[:8], refs[8:]
    copies = [
        pltpu.make_async_copy(src, dst, sems.at[i])
        for i, (src, dst) in enumerate(((mom_in, mom), (grad_in, grad), (q_in, q)))
    ]
    for copy in copies:
        copy.start()
    for copy in copies:
        copy.wait()
    buffer = mom[...] + grad[...].astype(f32)
    buf[...] = buffer
    total[...] = dot6(q[...], buffer, TT)
    half = total.shape[0] // 2
    for j in range(4):
        here = block_at(block_of(j), total.shape[1] // 4)
        parts[j][...] = total[:half, here]
        parts[4 + j][...] = total[half:, here]


def gather_blocks(pieces, out):
    for j, piece in enumerate(pieces):
        out[:, block_at(block_of(j), out.shape[1] // 4)] = piece[...]


def first_gram_kernel(p0, p1, p2, p3, upper, first):
    gather_blocks((p0, p1, p2, p3), upper)
    first[...] = dot6(upper[...], upper[...], NT)


def second_gram_kernel(p0, p1, p2, p3, upper, lower, second):
    gather_blocks((p0, p1, p2, p3), lower)
    half = lower.shape[0]
    second[:, :half] = dot6(lower[...], upper[...], NT)
    second[:, half:] = dot6(lower[...], lower[...], NT)


def first_cross_kernel(upper, buf, cross):
    cross[...] = dot6(buf[...], upper[...], NT)


def cross_kernel(lower, buf, cross, third):
    half = lower.shape[0]
    third[:, :half] = cross[...]
    third[:, half:] = dot6(buf[...], lower[...], NT)


def invert_factor(a):
    size = a.shape[0]
    groups = block_rows // 8
    lane = lax.broadcasted_iota(jnp.int32, (8, size), 1)
    row = lax.broadcasted_iota(jnp.int32, (8, size), 0)
    row_short = lax.broadcasted_iota(jnp.int32, (8, 128), 0)
    wide = size // 128

    def widen(x):
        return jnp.concatenate([x] * wide, axis=1) if wide > 1 else x

    def spread(x, s):
        return jnp.broadcast_to(x[s : s + 1, :], x.shape)

    for start in range(0, size, block_rows):
        panel = [a[start + 8 * g : start + 8 * g + 8, :] for g in range(groups)]
        pivots = [jnp.ones((8, 128), f32) for _ in range(groups)]
        for done in range(0, block_rows, step_rows):
            first = start + done
            cols = [
                {g: jnp.broadcast_to(panel[g][:, first + j : first + j + 1], (8, 128)) for g in range(done // 8, groups)}
                for j in range(step_rows)
            ]
            for g in range(groups):
                here = (lane >= first) & (lane < first + step_rows)
                panel[g] = jnp.where(here, jnp.where(lane - start == row + 8 * g, 1.0, 0.0), panel[g])
            for k in range(step_rows):
                top, s = divmod(done + k, 8)
                leads = {j: spread(cols[j][top], s) for j in range(k, step_rows)}
                inverse = 1.0 / leads[k]
                pivots[top] = jnp.where(row_short == s, leads[k], pivots[top])
                lead = spread(panel[top], s)
                for g in range(top, groups):
                    if g == top and s == 7:
                        continue
                    factor = cols[k][g] * inverse
                    for j in range(k + 1, step_rows):
                        cols[j][g] = cols[j][g] - factor * leads[j]
                    if g == top:
                        factor = jnp.where(row_short > s, factor, 0.0)
                    panel[g] = panel[g] - widen(factor) * lead
        rows = jnp.concatenate([panel[g] * widen(lax.rsqrt(pivots[g])) for g in range(groups)], axis=0)
        below = start + block_rows
        a[start:below, :] = rows
        if below < size:
            h, m, l = split3(rows)
            skip = below // 128 * 128
            left = jnp.concatenate([h, h, m, m, h, l], axis=0)[:, skip:]
            right = jnp.concatenate([h, m, h, m, l, h], axis=0)
            change = lax.dot_general(left, right, TT, preferred_element_type=f32)
            lanes = lax.broadcasted_iota(jnp.int32, (size - below, size), 1)
            here = (lanes >= start) & (lanes < below)
            a[below:, :] = jnp.where(here, 0.0, a[below:, :]) - change[below - skip :, :]
    i = lax.broadcasted_iota(jnp.int32, (size, size), 0)
    j = lax.broadcasted_iota(jnp.int32, (size, size), 1)
    a[...] = jnp.where(i >= j, a[...], 0.0)


def first_kernel(gram, came, inverse):
    inverse[...] = gram[...] + came[...]
    invert_factor(inverse)


def second_kernel(rest, came, inverse1, inverse, corner):
    half = inverse1.shape[0]
    inv1 = inverse1[...]
    gram = rest[...] + came[...]
    low = dot6(gram[:, :half], inv1, NT)
    corner[...] = gram[:, half:] - dot6(low, low, NT)
    below = dot6(low, inv1, NN)
    invert_factor(corner)
    inv2 = corner[...]
    inverse[:half, :half] = inv1
    inverse[:half, half:] = jnp.zeros_like(inv1)
    inverse[half:, :half] = -dot6(inv2, below, NN)
    inverse[half:, half:] = inv2


def right_kernel(cross, came, inverse, right, squares):
    r = dot6(cross[...] + came[...], inverse[...], NT)
    right[...] = r
    squares[...] = jnp.sum(r * r, axis=0, keepdims=True)


def ortho_kernel(upper, lower, inverse, ortho, high, mid):
    o = dot6(inverse[...], jnp.concatenate([upper[...], lower[...]], axis=0), NN)
    ortho[...] = o
    high[...], mid[...], _ = split3(o)


def momentum_kernel(buf, right, ortho, out):
    out[...] = buf[...] - (1.0 - momentum_decay) * dot6(right[...], ortho[...], NN)


def weight_kernel(scale, weight, right, squares, high, mid, out_hbm, q_hbm, out, q_new, sems):
    q = right[...] / (jnp.sqrt(squares[...]) + norm_eps)
    q_new[...] = q
    copies = [pltpu.make_async_copy(q_new, q_hbm, sems.at[2])]
    copies[0].start()
    qh, qm, _ = split3(q)

    def one(x, y):
        return lax.dot_general(x, y, NN, preferred_element_type=f32)

    half = out.shape[1] // 2
    for i in range(2):
        here = pl.ds(i * half, half)
        h, m = high[:, here], mid[:, here]
        update = one(qh, h) + (one(qh, m) + one(qm, h) + one(qm, m))
        out[:, here] = (weight[:, here].astype(f32) - scale * update).astype(bf16)
        copies.append(pltpu.make_async_copy(out.at[:, here], out_hbm.at[:, here], sems.at[i]))
        copies[-1].start()
    for copy in copies:
        copy.wait()


def per_device(fsdp, tensor, weight, momentum, grad, q_prev):
    cols, rows = momentum.shape
    rank = q_prev.shape[1]
    half = rank // 2
    scale = step_rate * math.sqrt(cols * tensor / (rows * fsdp))
    block = ((half, rows // 4), f32)
    buf, *parts = pl.pallas_call(
        power_kernel,
        out_shape=[jax.ShapeDtypeStruct(*x) for x in [((cols, rows), f32)] + [block] * 8],
        in_specs=[pl.BlockSpec(memory_space=pltpu.HBM)] * 3,
        out_specs=[pl.BlockSpec(memory_space=pltpu.VMEM)] * 9,
        scratch_shapes=[
            pltpu.VMEM((rank, rows), f32),
            pltpu.VMEM((cols, rows), f32),
            pltpu.VMEM((cols, rows), bf16),
            pltpu.VMEM((cols, rank), f32),
            pltpu.SemaphoreType.DMA((3,)),
        ],
        compiler_params=pltpu.CompilerParams(vmem_limit_bytes=vmem_bytes),
    )(*[pltpu.with_memory_space_constraint(x, pltpu.HBM) for x in (momentum, grad, q_prev)])
    totals = []
    for mine in (parts[:4], parts[4:]):
        came = [to_partner(mine[j], j, tensor) for j in (1, 2, 3)]
        totals.append(mine[0] + came[0] + came[1] + came[2])
    for bit in range(2, bits_of(tensor)):
        totals = [x + flip_tensor(x, bit, tensor) for x in totals]
    pieces = [[x] + [to_partner(x, j, tensor) for j in (1, 2, 3)] for x in totals]
    upper, first = call(first_gram_kernel, [((half, rows), f32), ((half, half), f32)], pieces[0])
    (cross,) = call(first_cross_kernel, [((cols, half), f32)], [upper, buf])
    cross, upper = lax.optimization_barrier((cross, upper))
    lower, second = call(second_gram_kernel, [((half, rows), f32), ((half, rank), f32)], [*pieces[1], upper])
    (third,) = call(cross_kernel, [((cols, rank), f32)], [lower, buf, cross])
    first = first + flip_fsdp(first, 0, fsdp)
    came = [flip_fsdp(x, 0, fsdp) for x in (second, third)]
    second, third = lax.optimization_barrier((second + came[0], third + came[1]))
    for bit in range(1, bits_of(fsdp) - 1):
        first, second, third = [x + flip_across(x, 1 << bit, 0, fsdp, tensor) for x in (first, second, third)]
    came = [flip_across(x, fsdp // 2, 0, fsdp, tensor) for x in (first, second, third)]
    (inverse1,) = call(first_kernel, [((half, half), f32)], [first, came[0]], micros=4)
    (inverse,) = call(second_kernel, [((rank, rank), f32)], [second, came[1], inverse1], [(half, half)], micros=4)
    right, squares = call(right_kernel, [((cols, rank), f32), ((1, rank), f32)], [third, came[2], inverse])
    ortho, high, mid = call(
        ortho_kernel,
        [((rank, rows), f32), ((rank, rows), bf16), ((rank, rows), bf16)],
        [upper, lower, inverse],
    )
    (new_momentum,) = call(momentum_kernel, [((cols, rows), f32)], [buf, right, ortho], micros=2)
    came = [flip_across(squares, 0, j, fsdp, tensor) for j in (3, 1, 2)]
    squares = squares + came[0] + came[1] + came[2]
    squares, ortho = lax.optimization_barrier((squares, ortho))
    for bit in range(2, bits_of(tensor)):
        squares = squares + flip_across(squares, 0, 1 << bit, fsdp, tensor)
    new_weight, q_new = pl.pallas_call(
        functools.partial(weight_kernel, scale),
        out_shape=[jax.ShapeDtypeStruct((cols, rows), bf16), jax.ShapeDtypeStruct((cols, rank), f32)],
        in_specs=[pl.BlockSpec(memory_space=pltpu.VMEM)] * 5,
        out_specs=[pl.BlockSpec(memory_space=pltpu.HBM)] * 2,
        scratch_shapes=[
            pltpu.VMEM((cols, rows), bf16),
            pltpu.VMEM((cols, rank), f32),
            pltpu.SemaphoreType.DMA((3,)),
        ],
        compiler_params=pltpu.CompilerParams(vmem_limit_bytes=vmem_bytes),
    )(weight, right, squares, high, mid)
    return (new_weight, new_momentum, q_new)


def solution(mesh):
    placed = (P("tensor", "fsdp"), P("tensor", "fsdp"), P("tensor", "fsdp"), P("tensor", None))
    return jax.shard_map(
        functools.partial(per_device, mesh.shape["fsdp"], mesh.shape["tensor"]),
        mesh=mesh,
        in_specs=placed,
        out_specs=(P("tensor", "fsdp"), P("tensor", "fsdp"), P("tensor", None)),
        check_vma=False,
    )
```

```python
import functools
import math

import jax
import jax.numpy as jnp
from jax import lax
from jax.experimental import pallas as pl
from jax.experimental.pallas import tpu as pltpu
from jax.sharding import PartitionSpec as P

momentum_decay = 0.95
step_rate = 0.02
norm_eps = 1e-06
f32 = jnp.float32
bf16 = jnp.bfloat16
block_rows = 32
step_rows = 16
vmem_bytes = 32 * 1024 * 1024
TT = (((0,), (0,)), ((), ()))
NN = (((1,), (0,)), ((), ()))
NT = (((1,), (1,)), ((), ()))


def split3(x):
    high = x.astype(bf16)
    rest = x - high.astype(f32)
    mid = rest.astype(bf16)
    return high, mid, (rest - mid.astype(f32)).astype(bf16)


def dot6(a, b, dims):
    ah, am, al = split3(a)
    bh, bm, bl = split3(b)
    (a_dim,), (b_dim,) = dims[0]
    left = jnp.concatenate([ah, ah, am, am, ah, al], axis=a_dim)
    right = jnp.concatenate([bh, bm, bh, bm, bl, bh], axis=b_dim)
    return lax.dot_general(left, right, dims, preferred_element_type=f32)


def bits_of(size):
    return size.bit_length() - 1


def partner(j):
    return (0, 3, 1, 2)[j]


def block_of(j):
    return (lax.axis_index("tensor") % 4) ^ partner(j)


def to_partner(x, j, tensor):
    return lax.ppermute(x, "tensor", [(t, t ^ partner(j)) for t in range(tensor)])


def flip_tensor(x, bit, tensor):
    return lax.ppermute(x, "tensor", [(t, t ^ (1 << bit)) for t in range(tensor)])


def flip_fsdp(x, bit, fsdp):
    return lax.ppermute(x, "fsdp", [(f, f ^ (1 << bit)) for f in range(fsdp)])


def flip_across(x, f_flip, t_flip, fsdp, tensor):
    pairs = []
    for f in range(fsdp):
        for t in range(tensor):
            pairs.append((f * tensor + t, (f ^ 1 ^ f_flip) * tensor + (t ^ t_flip)))
    return lax.ppermute(x, ("fsdp", "tensor"), pairs)


def call(body, outs, ins, scratch=(), micros=1):
    shapes = [jax.ShapeDtypeStruct(shape, dtype) for shape, dtype in outs]
    return pl.pallas_call(
        body,
        out_shape=shapes,
        in_specs=[pl.BlockSpec(memory_space=pltpu.VMEM)] * len(ins),
        out_specs=[pl.BlockSpec(memory_space=pltpu.VMEM)] * len(outs),
        scratch_shapes=[pltpu.VMEM(shape, f32) for shape in scratch],
        compiler_params=pltpu.CompilerParams(vmem_limit_bytes=vmem_bytes),
        cost_estimate=pl.CostEstimate(flops=int(micros * 1e9), bytes_accessed=0, transcendentals=0),
    )(*ins)


def block_at(index, size):
    return pl.ds(pl.multiple_of(index * size, size), size)


def power_kernel(mom_in, grad_in, q_in, buf, *refs):
    parts, (total, mom, grad, q, sems) = refs[:8], refs[8:]
    copies = [
        pltpu.make_async_copy(src, dst, sems.at[i])
        for i, (src, dst) in enumerate(((mom_in, mom), (grad_in, grad), (q_in, q)))
    ]
    for copy in copies:
        copy.start()
    for copy in copies:
        copy.wait()
    buffer = mom[...] + grad[...].astype(f32)
    buf[...] = buffer
    total[...] = dot6(q[...], buffer, TT)
    half = total.shape[0] // 2
    for j in range(4):
        here = block_at(block_of(j), total.shape[1] // 4)
        parts[j][...] = total[:half, here]
        parts[4 + j][...] = total[half:, here]


def gather_blocks(pieces, out):
    for j, piece in enumerate(pieces):
        out[:, block_at(block_of(j), out.shape[1] // 4)] = piece[...]


def first_gram_kernel(p0, p1, p2, p3, upper, first):
    gather_blocks((p0, p1, p2, p3), upper)
    first[...] = dot6(upper[...], upper[...], NT)


def second_gram_kernel(p0, p1, p2, p3, upper, lower, second):
    gather_blocks((p0, p1, p2, p3), lower)
    half = lower.shape[0]
    second[:, :half] = dot6(lower[...], upper[...], NT)
    second[:, half:] = dot6(lower[...], lower[...], NT)


def first_cross_kernel(upper, buf, cross):
    cross[...] = dot6(buf[...], upper[...], NT)


def cross_kernel(lower, buf, cross, third):
    half = lower.shape[0]
    third[:, :half] = cross[...]
    third[:, half:] = dot6(buf[...], lower[...], NT)


def invert_factor(a):
    size = a.shape[0]
    groups = block_rows // 8
    lane = lax.broadcasted_iota(jnp.int32, (8, size), 1)
    row = lax.broadcasted_iota(jnp.int32, (8, size), 0)
    row_short = lax.broadcasted_iota(jnp.int32, (8, 128), 0)
    wide = size // 128

    def widen(x):
        return jnp.concatenate([x] * wide, axis=1) if wide > 1 else x

    def spread(x, s):
        return jnp.broadcast_to(x[s : s + 1, :], x.shape)

    for start in range(0, size, block_rows):
        panel = [a[start + 8 * g : start + 8 * g + 8, :] for g in range(groups)]
        pivots = [jnp.ones((8, 128), f32) for _ in range(groups)]
        for done in range(0, block_rows, step_rows):
            first = start + done
            cols = [
                {g: jnp.broadcast_to(panel[g][:, first + j : first + j + 1], (8, 128)) for g in range(done // 8, groups)}
                for j in range(step_rows)
            ]
            for g in range(groups):
                here = (lane >= first) & (lane < first + step_rows)
                panel[g] = jnp.where(here, jnp.where(lane - start == row + 8 * g, 1.0, 0.0), panel[g])
            for k in range(step_rows):
                top, s = divmod(done + k, 8)
                leads = {j: spread(cols[j][top], s) for j in range(k, step_rows)}
                inverse = 1.0 / leads[k]
                pivots[top] = jnp.where(row_short == s, leads[k], pivots[top])
                lead = spread(panel[top], s)
                for g in range(top, groups):
                    if g == top and s == 7:
                        continue
                    factor = cols[k][g] * inverse
                    for j in range(k + 1, step_rows):
                        cols[j][g] = cols[j][g] - factor * leads[j]
                    if g == top:
                        factor = jnp.where(row_short > s, factor, 0.0)
                    panel[g] = panel[g] - widen(factor) * lead
        rows = jnp.concatenate([panel[g] * widen(lax.rsqrt(pivots[g])) for g in range(groups)], axis=0)
        below = start + block_rows
        a[start:below, :] = rows
        if below < size:
            h, m, l = split3(rows)
            skip = below // 128 * 128
            left = jnp.concatenate([h, h, m, m, h, l], axis=0)[:, skip:]
            right = jnp.concatenate([h, m, h, m, l, h], axis=0)
            change = lax.dot_general(left, right, TT, preferred_element_type=f32)
            lanes = lax.broadcasted_iota(jnp.int32, (size - below, size), 1)
            here = (lanes >= start) & (lanes < below)
            a[below:, :] = jnp.where(here, 0.0, a[below:, :]) - change[below - skip :, :]
    i = lax.broadcasted_iota(jnp.int32, (size, size), 0)
    j = lax.broadcasted_iota(jnp.int32, (size, size), 1)
    a[...] = jnp.where(i >= j, a[...], 0.0)


def first_kernel(gram, came, inverse):
    inverse[...] = gram[...] + came[...]
    invert_factor(inverse)


def second_kernel(rest, came, inverse1, inverse, corner):
    half = inverse1.shape[0]
    inv1 = inverse1[...]
    gram = rest[...] + came[...]
    low = dot6(gram[:, :half], inv1, NT)
    corner[...] = gram[:, half:] - dot6(low, low, NT)
    below = dot6(low, inv1, NN)
    invert_factor(corner)
    inv2 = corner[...]
    inverse[:half, :half] = inv1
    inverse[:half, half:] = jnp.zeros_like(inv1)
    inverse[half:, :half] = -dot6(inv2, below, NN)
    inverse[half:, half:] = inv2


def right_kernel(cross, came, inverse, right, squares):
    r = dot6(cross[...] + came[...], inverse[...], NT)
    right[...] = r
    squares[...] = jnp.sum(r * r, axis=0, keepdims=True)


def ortho_kernel(upper, lower, inverse, ortho, high, mid):
    o = dot6(inverse[...], jnp.concatenate([upper[...], lower[...]], axis=0), NN)
    ortho[...] = o
    high[...], mid[...], _ = split3(o)


def momentum_kernel(buf, right, ortho, out):
    out[...] = buf[...] - (1.0 - momentum_decay) * dot6(right[...], ortho[...], NN)


def weight_kernel(scale, weight, right, squares, high, mid, out_hbm, q_hbm, out, q_new, sems):
    q = right[...] / (jnp.sqrt(squares[...]) + norm_eps)
    q_new[...] = q
    copies = [pltpu.make_async_copy(q_new, q_hbm, sems.at[2])]
    copies[0].start()
    qh, qm, _ = split3(q)

    def one(x, y):
        return lax.dot_general(x, y, NN, preferred_element_type=f32)

    half = out.shape[1] // 2
    for i in range(2):
        here = pl.ds(i * half, half)
        h, m = high[:, here], mid[:, here]
        update = one(qh, h) + (one(qh, m) + one(qm, h) + one(qm, m))
        out[:, here] = (weight[:, here].astype(f32) - scale * update).astype(bf16)
        copies.append(pltpu.make_async_copy(out.at[:, here], out_hbm.at[:, here], sems.at[i]))
        copies[-1].start()
    for copy in copies:
        copy.wait()


def per_device(fsdp, tensor, weight, momentum, grad, q_prev):
    cols, rows = momentum.shape
    rank = q_prev.shape[1]
    half = rank // 2
    scale = step_rate * math.sqrt(cols * tensor / (rows * fsdp))
    block = ((half, rows // 4), f32)
    buf, *parts = pl.pallas_call(
        power_kernel,
        out_shape=[jax.ShapeDtypeStruct(*x) for x in [((cols, rows), f32)] + [block] * 8],
        in_specs=[pl.BlockSpec(memory_space=pltpu.HBM)] * 3,
        out_specs=[pl.BlockSpec(memory_space=pltpu.VMEM)] * 9,
        scratch_shapes=[
            pltpu.VMEM((rank, rows), f32),
            pltpu.VMEM((cols, rows), f32),
            pltpu.VMEM((cols, rows), bf16),
            pltpu.VMEM((cols, rank), f32),
            pltpu.SemaphoreType.DMA((3,)),
        ],
        compiler_params=pltpu.CompilerParams(vmem_limit_bytes=vmem_bytes),
    )(*[pltpu.with_memory_space_constraint(x, pltpu.HBM) for x in (momentum, grad, q_prev)])
    totals = []
    for mine in (parts[:4], parts[4:]):
        came = [to_partner(mine[j], j, tensor) for j in (1, 2, 3)]
        totals.append(mine[0] + came[0] + came[1] + came[2])
    for bit in range(2, bits_of(tensor)):
        totals = [x + flip_tensor(x, bit, tensor) for x in totals]
    pieces = [[x] + [to_partner(x, j, tensor) for j in (1, 2, 3)] for x in totals]
    upper, first = call(first_gram_kernel, [((half, rows), f32), ((half, half), f32)], pieces[0])
    (cross,) = call(first_cross_kernel, [((cols, half), f32)], [upper, buf])
    cross, upper = lax.optimization_barrier((cross, upper))
    lower, second = call(second_gram_kernel, [((half, rows), f32), ((half, rank), f32)], [*pieces[1], upper])
    (third,) = call(cross_kernel, [((cols, rank), f32)], [lower, buf, cross])
    first = first + flip_fsdp(first, 0, fsdp)
    came = [flip_fsdp(x, 0, fsdp) for x in (second, third)]
    second, third = lax.optimization_barrier((second + came[0], third + came[1]))
    for bit in range(1, bits_of(fsdp) - 1):
        first, second, third = [x + flip_across(x, 1 << bit, 0, fsdp, tensor) for x in (first, second, third)]
    came = [flip_across(x, fsdp // 2, 0, fsdp, tensor) for x in (first, second)]
    came.append(flip_fsdp(third, bits_of(fsdp) - 1, fsdp))
    (inverse1,) = call(first_kernel, [((half, half), f32)], [first, came[0]], micros=4)
    (inverse,) = call(second_kernel, [((rank, rank), f32)], [second, came[1], inverse1], [(half, half)], micros=4)
    right, squares = call(right_kernel, [((cols, rank), f32), ((1, rank), f32)], [third, came[2], inverse])
    ortho, high, mid = call(
        ortho_kernel,
        [((rank, rows), f32), ((rank, rows), bf16), ((rank, rows), bf16)],
        [upper, lower, inverse],
    )
    (new_momentum,) = call(momentum_kernel, [((cols, rows), f32)], [buf, right, ortho], micros=2)
    came = [flip_across(squares, 0, j, fsdp, tensor) for j in (3, 1, 2)]
    squares = squares + came[0] + came[1] + came[2]
    squares, ortho = lax.optimization_barrier((squares, ortho))
    for bit in range(2, bits_of(tensor)):
        squares = squares + flip_across(squares, 0, 1 << bit, fsdp, tensor)
    new_weight, q_new = pl.pallas_call(
        functools.partial(weight_kernel, scale),
        out_shape=[jax.ShapeDtypeStruct((cols, rows), bf16), jax.ShapeDtypeStruct((cols, rank), f32)],
        in_specs=[pl.BlockSpec(memory_space=pltpu.VMEM)] * 5,
        out_specs=[pl.BlockSpec(memory_space=pltpu.HBM)] * 2,
        scratch_shapes=[
            pltpu.VMEM((cols, rows), bf16),
            pltpu.VMEM((cols, rank), f32),
            pltpu.SemaphoreType.DMA((3,)),
        ],
        compiler_params=pltpu.CompilerParams(vmem_limit_bytes=vmem_bytes),
    )(weight, right, squares, high, mid)
    return (new_weight, new_momentum, q_new)


def solution(mesh):
    placed = (P("tensor", "fsdp"), P("tensor", "fsdp"), P("tensor", "fsdp"), P("tensor", None))
    return jax.shard_map(
        functools.partial(per_device, mesh.shape["fsdp"], mesh.shape["tensor"]),
        mesh=mesh,
        in_specs=placed,
        out_specs=(P("tensor", "fsdp"), P("tensor", "fsdp"), P("tensor", None)),
        check_vma=False,
    )
```
